32 devices in a mesh: groups: 2 (over y), dp: 4 (over z), tensor: 4 (over x, core).
Axes of the slice: x: 2, y: 2, z: 4, core: 2. Of those that a mesh axis runs over, the one named last changes fastest.
Arguments:
- tokens: bfloat16 [2048, 16384], P(('groups', 'dp', 'tensor')), parts along dimension 0, may hold values from -6 to 6
- up_weight: bfloat16 [16384, 26624], P('dp', 'tensor'), may hold values from -0.046875 to 0.046875
- adapter_down: bfloat16 [8, 64, 16384], P('groups', None, ('dp', 'tensor')), parts along dimension 0, may hold values from -0.046875 to 0.046875
- adapter_up: bfloat16 [8, 64, 26624], P('groups', None, 'tensor'), parts along dimension 0, may hold values from -0.75 to 0.75
- grad_out: bfloat16 [2048, 26624], P(('groups', 'dp'), 'tensor'), parts along dimension 0, may hold values from -0.29882812 to 0.29882812
- block_tenant: int32 [16], P('groups'), parts along dimension 0, may hold values from 0 to 3, as said below
- owner_of: int32 [8], P('groups'), parts along dimension 0, may hold values from 0 to 3, as said below
Outputs:
- layer_out: bfloat16 [2048, 26624], P(('groups', 'dp'), 'tensor'), parts along dimension 0
- grad_down: float32 [8, 64, 16384], P('groups', None, ('dp', 'tensor')), parts along dimension 0
- grad_up: float32 [16, 64, 26624], P(('groups', 'dp'), None, 'tensor'), parts along dimension 0
The draws below stay inside these ranges and needn't reach their ends.
There are 2 independent parts, one for each index of `groups`. The reference program is written for one: setup_inputs(seed, part) draws one part's arguments, and reference() takes and returns one part's arrays. A program takes and returns all parts, laid end to end along the dimension named above; an argument that names none is the same for every part. Nothing has to cross between parts.
Inputs may be any that keep to these rules, and one draw needn't show every extreme that they name: `block_tenant`: tenant numbers never fall along the blocks; every tenant names 1 to 3 blocks in a row, and some tenant names exactly 3. `owner_of`: no owner is named by more than 2 tenants; one owner is named by exactly 2.
All inputs are finite; a program needn't handle non-finite values.
Results may differ from the reference program's by a relative error of at most 0.01.
Values may be sent and summed in bfloat16 or wider, within the bound.
No kernel may reach another device: no remote copies, remote signals or barrier semaphores. Data moves between devices by JAX's collectives and lax.ppermute only.
A program may use at most 256 MiB of HBM per device.

```python
import jax
import jax.numpy as jnp
from jax import lax

D = 16384
FF = 26624
RANK = 64
ROWS_BLK = 128
OWN_MAX = 2
OWNERS = 4
SLOTS = 8
NBLK = 8
TENANTS = 4
TOKENS = 1024
N_DP = 4


def draw_block_tenant(key, part):
    key = jax.random.fold_in(key, 3)
    pair_key, order_key = jax.random.split(key)
    halves = TENANTS // 2
    firsts = jax.random.randint(pair_key, (halves,), 1, 4).astype(jnp.int32)
    firsts = firsts.at[0].set(3)
    counts = jnp.stack([firsts, 4 - firsts], axis=1).reshape(TENANTS)
    order = jax.random.permutation(order_key, TENANTS)
    counts = counts[order].astype(jnp.int32)
    target = jnp.where(part % 2 == 0, 3, 1).astype(jnp.int32)
    found = jnp.argmax(counts == target).astype(jnp.int32)
    leading = counts[0]
    counts = counts.at[found].set(leading).at[0].set(target).astype(jnp.int32)
    ends = jnp.cumsum(counts)
    blocks = jnp.arange(NBLK, dtype=jnp.int32)
    return jnp.sum((blocks[:, None] >= ends[None, :]).astype(jnp.int32), axis=1).astype(jnp.int32)


def draw_owner_of(key, part):
    key = jax.random.fold_in(key, 7)
    star_key, slot_key, order_key = jax.random.split(key, 3)
    star = jax.random.randint(star_key, (), 0, OWNERS).astype(jnp.int32)
    others = jax.random.permutation(slot_key, (OWNERS - 1) * OWN_MAX)[:TENANTS - OWN_MAX].astype(jnp.int32)
    other_owner = (star + 1 + others // OWN_MAX) % OWNERS
    by_rank = jnp.concatenate([jnp.zeros((OWN_MAX,), jnp.int32) + star, other_owner])
    order = jax.random.permutation(order_key, TENANTS)
    return by_rank[order].astype(jnp.int32)


def shard_levels(rng, dims, pieces, low, high):
    level, own = 1.0, jax.random.fold_in(rng, 6)
    for axis_at, parts in pieces:
        draws = jnp.exp(jax.random.uniform(jax.random.fold_in(own, axis_at), (parts,), jnp.float32, low / len(pieces), high / len(pieces)))
        level = level * jnp.repeat(draws, dims[axis_at] // parts).reshape([-1 if axis == axis_at else 1 for axis in range(len(dims))])
    return level


def noise(key, extent, spread, most, pieces=(), held_as=jnp.bfloat16):
    entries = spread * jax.random.normal(key, extent, jnp.float32)
    if pieces:
        entries = entries * shard_levels(key, extent, pieces, -0.22, 0.18)
    return jnp.clip(entries, -most, most).astype(held_as)


def setup_inputs(seed: int = 0, part: int = 0) -> dict:
    key_list = jax.random.split(jax.random.key(seed), 8)
    part_splits = jax.random.split(jax.random.fold_in(key_list[7], part), 8)
    return {
        "tokens": noise(part_splits[0], (TOKENS, D), 1.0, 6.0, ((0, 16),)),
        "up_weight": noise(key_list[1], (D, FF), D ** -0.5, 0.046875, ((0, 4), (1, 4))),
        "adapter_down": noise(part_splits[2], (TENANTS, RANK, D), D ** -0.5, 0.046875, ((2, 16),)),
        "adapter_up": noise(part_splits[3], (TENANTS, RANK, FF), RANK ** -0.5, 0.75, ((2, 4),)),
        "grad_out": noise(part_splits[4], (TOKENS, FF), 0.05, 0.29882812, ((0, 4), (1, 4))),
        "block_tenant": draw_block_tenant(jax.random.fold_in(jax.random.fold_in(key_list[7], part), 71), part),
        "owner_of": draw_owner_of(jax.random.fold_in(jax.random.fold_in(key_list[7], part), 71), part),
    }


SCALE = 0.5


def reference(tokens, up_weight, adapter_down, adapter_up, grad_out, block_tenant, owner_of):
    column_part = D // N_DP
    base_out = jnp.zeros((TOKENS, FF), jnp.float32)
    for block_index in range(N_DP):
        first_col = block_index * column_part
        partial_value = jnp.dot(tokens[:, first_col:first_col + column_part], up_weight[first_col:first_col + column_part], preferred_element_type=jnp.float32)
        rounded = lax.optimization_barrier(partial_value.astype(jnp.bfloat16))
        base_out = base_out + rounded.astype(jnp.float32)
    features = tokens.reshape(NBLK, ROWS_BLK, D).astype(jnp.float32)
    down_blocks = adapter_down[block_tenant].astype(jnp.float32)
    up_blocks = adapter_up[block_tenant].astype(jnp.float32)
    out_blocks = grad_out.reshape(NBLK, ROWS_BLK, FF).astype(jnp.float32)
    projected = jnp.einsum('nrd,nkd->nrk', features, down_blocks).astype(jnp.bfloat16)
    adapter_term = jnp.einsum('nrk,nkf->nrf', projected.astype(jnp.float32), up_blocks)
    layer_out = (base_out + SCALE * adapter_term.reshape(TOKENS, FF)).astype(jnp.bfloat16)
    back_proj = (SCALE * jnp.einsum('nrf,nkf->nrk', out_blocks, up_blocks)).astype(jnp.bfloat16)
    down_terms = jnp.einsum('nrk,nrd->nkd', back_proj.astype(jnp.float32), features)
    up_terms = SCALE * jnp.einsum('nrk,nrf->nkf', projected.astype(jnp.float32), out_blocks)
    tenant_ids = jnp.arange(TENANTS, dtype=jnp.int32)
    onehot = (block_tenant[None, :] == tenant_ids[:, None]).astype(jnp.float32)
    inverse = 1.0 / jnp.sum(onehot, axis=1)
    grad_down = jnp.einsum('tn,nkd->tkd', onehot, down_terms, precision=lax.Precision.HIGHEST) * inverse[:, None, None]
    up_tenant = jnp.einsum('tn,nkf->tkf', onehot, up_terms, precision=lax.Precision.HIGHEST) * inverse[:, None, None]
    same_owner = owner_of[:, None] == owner_of[None, :]
    earlier = tenant_ids[None, :] < tenant_ids[:, None]
    rank_in = jnp.sum(jnp.logical_and(same_owner, earlier), axis=1).astype(jnp.int32)
    slot_of = owner_of * OWN_MAX + rank_in
    placement = (slot_of[None, :] == jnp.arange(SLOTS, dtype=jnp.int32)[:, None]).astype(jnp.float32)
    grad_up = jnp.einsum('st,tkf->skf', placement, up_tenant, precision=lax.Precision.HIGHEST)
    return (layer_out, grad_down, grad_up)
```

```python
import functools

import jax
import jax.numpy as jnp
from jax import lax
from jax.experimental import pallas as pl
from jax.experimental.pallas import tpu as pltpu
from jax.sharding import PartitionSpec as P

ROWS_BLK = 128
OWN_MAX = 2
SCALE = 0.5
SPLIT = ((0, 2), (2, 5), (5, 9), (9, 13))
WINDOW = 3
VMEM = 40 * 1024 * 1024
ANY = pl.BlockSpec(memory_space=pl.ANY)
SMEM = pl.BlockSpec(memory_space=pltpu.SMEM)


def after(value, *earlier):
    return lax.optimization_barrier((value, *earlier))[0]


def across(value, axis, bit):
    count = lax.axis_size(axis)
    return lax.ppermute(value, axis, [(i, i ^ bit) for i in range(count)])


def outward(value, hop):
    last = lax.axis_size("dp") - 1
    return lax.ppermute(value, "dp", [(hop, hop + 1), (last - hop, last - hop - 1)])


def bits_of(count):
    return [1 << k for k in reversed(range(count.bit_length() - 1))]


def gather_rows(rows):
    held = [(0, rows)]
    for bit in bits_of(lax.axis_size("tensor")):
        held = held + [(mask | bit, across(value, "tensor", bit)) for mask, value in held]
    return held


def sum_over_tensor(value):
    for bit in bits_of(lax.axis_size("tensor")):
        value = value + across(value, "tensor", bit)
    return value


def tile_of(width):
    return 512 if width % 512 == 0 else 128


def cut(width):
    tiles = width // tile_of(width)
    counts = [tiles * (i + 1) // 13 - tiles * i // 13 for i in range(13)]
    counts = [sum(counts[a:b]) for a, b in SPLIT]
    edges = [0]
    for n in counts:
        edges.append(edges[-1] + n)
    return list(zip(edges[:-1], counts))


def call(kernel, flops, **kwargs):
    return pl.pallas_call(
        kernel,
        compiler_params=pltpu.CompilerParams(vmem_limit_bytes=VMEM),
        cost_estimate=pl.CostEstimate(flops=flops, bytes_accessed=0, transcendentals=0),
        **kwargs,
    )


def share_kernel(masks, has_add, deps, index, *refs):
    blocks, refs = refs[: len(masks)], refs[len(masks) :]
    weight, refs = refs[0], refs[1:]
    if has_add:
        arrived, refs = refs[0], refs[1:]
    refs = refs[deps:]
    rows = blocks[0].shape[0]
    batch = refs[-1]

    @pl.when(pl.program_id(0) == 0)
    def _():
        for mask, block in zip(masks, blocks):
            first = pl.multiple_of((index[0] ^ mask) * rows, rows)
            batch[pl.ds(first, rows), :] = block[...]

    value = jnp.dot(batch[...], weight[...], preferred_element_type=jnp.float32)
    refs[0][...] = value.astype(jnp.bfloat16)
    if has_add:
        refs[1][...] = (value + arrived[...].astype(jnp.float32)).astype(jnp.bfloat16)


def share(index, gathered, weight, piece, arrived=None, deps=()):
    masks, blocks = zip(*gathered)
    rows, depth = blocks[0].shape
    batch_rows = rows * len(blocks)
    tile = tile_of(weight.shape[1])
    first, count = piece
    out = jax.ShapeDtypeStruct((batch_rows, count * tile), jnp.bfloat16)
    column = pl.BlockSpec((batch_rows, tile), lambda i, s: (0, i))
    has_add = arrived is not None
    result = call(
        functools.partial(share_kernel, masks, has_add, len(deps)),
        2 * batch_rows * depth * count * tile,
        out_shape=[out] * (1 + has_add),
        grid_spec=pltpu.PrefetchScalarGridSpec(
            num_scalar_prefetch=1,
            grid=(count,),
            in_specs=[pl.BlockSpec((rows, depth), lambda i, s: (0, 0))] * len(blocks)
            + [pl.BlockSpec((depth, tile), lambda i, s: (0, first + i))]
            + [column] * has_add
            + [ANY] * len(deps),
            out_specs=[column] * (1 + has_add),
            scratch_shapes=[pltpu.VMEM((batch_rows, depth), jnp.bfloat16)],
        ),
    )(index, *blocks, weight, *([arrived] if has_add else []), *deps)
    return result if has_add else result[0]


def forward_kernel(masks, batches, index, ids, *refs):
    blocks, refs = refs[: batches * len(masks)], refs[batches * len(masks) :]
    down, features, parts = refs[0], refs[1], refs[2:]
    rows = blocks[0].shape[0]
    batch_rows = rows * len(masks)
    local_blocks = batch_rows // ROWS_BLK
    for d in range(batches):
        for k, mask in enumerate(masks):
            first = pl.multiple_of(d * batch_rows + (index[0] ^ mask) * rows, rows)
            features[pl.ds(first, rows), :] = blocks[d * len(masks) + k][...]
        for b in range(local_blocks):
            first = d * batch_rows + b * ROWS_BLK
            parts[d][b * ROWS_BLK : (b + 1) * ROWS_BLK, :] = lax.dot_general(
                features[first : first + ROWS_BLK, :],
                down[ids[d * local_blocks + b]],
                (((1,), (1,)), ((), ())),
                preferred_element_type=jnp.float32,
            )


def forward(index, ids, gathered, adapter_down):
    batches = len(gathered)
    masks = [mask for mask, _ in gathered[0]]
    rows = gathered[0][0][1].shape[0]
    batch_rows = rows * len(masks)
    rank_width, slice_cols = adapter_down.shape[1:]
    return call(
        functools.partial(forward_kernel, masks, batches),
        2 * batches * batch_rows * slice_cols * rank_width * 4,
        out_shape=[jax.ShapeDtypeStruct((batches * batch_rows, slice_cols), jnp.bfloat16)]
        + [jax.ShapeDtypeStruct((batch_rows, rank_width), jnp.float32)] * batches,
        grid_spec=pltpu.PrefetchScalarGridSpec(
            num_scalar_prefetch=2,
            grid=(1,),
            in_specs=[pl.BlockSpec((rows, slice_cols), lambda i, s, n: (0, s[0]))] * (batches * len(masks))
            + [pl.BlockSpec(adapter_down.shape, lambda i, s, n: (0, 0, 0))],
            out_specs=[pl.BlockSpec((batches * batch_rows, slice_cols), lambda i, s, n: (0, 0))]
            + [pl.BlockSpec((batch_rows, rank_width), lambda i, s, n: (0, 0))] * batches,
        ),
    )(index, ids, *[value for d in range(batches) for _, value in gathered[d]], adapter_down)


def backward_kernel(ids, grad, up, out):
    @pl.when(pl.program_id(0) == 0)
    def _():
        out[...] = jnp.zeros_like(out)

    for b in range(grad.shape[0] // ROWS_BLK):
        rows = slice(b * ROWS_BLK, (b + 1) * ROWS_BLK)
        out[rows, :] += lax.dot_general(
            grad[rows, :], up[ids[b]], (((1,), (1,)), ((), ())), preferred_element_type=jnp.float32
        )


def backward(ids, grad_out, adapter_up):
    batch_rows, hidden = grad_out.shape
    tenants, rank_width, _ = adapter_up.shape
    tile = tile_of(hidden)
    return call(
        backward_kernel,
        2 * batch_rows * hidden * rank_width * 4,
        out_shape=jax.ShapeDtypeStruct((batch_rows, rank_width), jnp.float32),
        grid_spec=pltpu.PrefetchScalarGridSpec(
            num_scalar_prefetch=1,
            grid=(hidden // tile,),
            in_specs=[
                pl.BlockSpec((batch_rows, tile), lambda i, n: (0, i)),
                pl.BlockSpec((tenants, rank_width, tile), lambda i, n: (0, 0, i)),
            ],
            out_specs=pl.BlockSpec((batch_rows, rank_width), lambda i, n: (0, 0)),
        ),
    )(ids, grad_out, adapter_up)


def down_kernel(batches, ids, inverse, features, *refs):
    backs, out = refs[:batches], refs[batches]
    batch_rows = backs[0].shape[0]
    local_blocks = batch_rows // ROWS_BLK
    out[...] = jnp.zeros_like(out)
    for d in range(batches):
        for b in range(local_blocks):
            first = d * batch_rows + b * ROWS_BLK
            tenant = ids[d * local_blocks + b]
            out[tenant] += lax.dot_general(
                backs[d][b * ROWS_BLK : (b + 1) * ROWS_BLK, :],
                features[first : first + ROWS_BLK, :],
                (((0,), (0,)), ((), ())),
                preferred_element_type=jnp.float32,
            )
    for n in range(out.shape[0]):
        out[n] *= inverse[n]


def down_gradient(ids, inverse, features, backs, shape):
    whole = pl.BlockSpec(memory_space=pltpu.VMEM)
    return call(
        functools.partial(down_kernel, len(backs)),
        2 * features.size * backs[0].shape[1] * 4,
        out_shape=jax.ShapeDtypeStruct(shape, jnp.float32),
        in_specs=[SMEM, SMEM] + [whole] * (1 + len(backs)),
        out_specs=whole,
    )(ids, inverse, features, *backs)


def combine_kernel(count, extras, weights, scale, *refs):
    terms, more, out = refs[:count], refs[count : count + extras], refs[count + extras]
    parts = [term[0].astype(jnp.float32) for term in terms]
    for s in range(out.shape[0]):
        total = sum(part * weights[s, n] for n, part in enumerate(parts))
        if extras:
            total += sum(extra[s].astype(jnp.float32) for extra in more) * scale[s]
        out[s] = total.astype(out.dtype)


def combine(weights, terms, dtype, scale=None, extras=()):
    rank_width, hidden = terms[0].shape[1:]
    tile = tile_of(hidden)
    slots = weights.shape[0]
    if scale is None:
        scale = jnp.ones((slots,), jnp.float32)
    return call(
        functools.partial(combine_kernel, len(terms), len(extras)),
        4 * slots * rank_width * hidden * len(terms),
        out_shape=jax.ShapeDtypeStruct((slots, rank_width, hidden), dtype),
        grid=(hidden // tile,),
        in_specs=[SMEM, SMEM]
        + [pl.BlockSpec((1, rank_width, tile), lambda i: (0, 0, i))] * len(terms)
        + [pl.BlockSpec((slots, rank_width, tile), lambda i: (0, 0, i))] * len(extras),
        out_specs=pl.BlockSpec((slots, rank_width, tile), lambda i: (0, 0, i)),
    )(weights, scale, *terms, *extras)


def local(tokens, up_weight, adapter_down, adapter_up, grad_out, block_tenant, owner_of):
    dp_count = 4
    z = lax.axis_index("dp")
    t = lax.axis_index("tensor")
    outer = jnp.logical_or(z == 0, z == 3)
    feature_count = tokens.shape[1]
    batch_rows, hidden = grad_out.shape
    local_blocks = batch_rows // ROWS_BLK
    depth = feature_count // dp_count
    tenants, rank_width, slice_cols = adapter_down.shape
    flat_up = adapter_up.reshape(tenants * rank_width, hidden)
    pieces = cut(hidden)
    tile = tile_of(hidden)
    index = t.reshape(1)

    def block_for(where):
        return lax.dynamic_slice_in_dim(tokens, where * depth, depth, 1)

    far = lax.ppermute(block_for(z ^ 3), "dp", [(0, 3), (3, 0)])
    middle = lax.ppermute(block_for(z ^ 3), "dp", [(1, 2), (2, 1)])
    two = across(block_for(z ^ 2), "dp", 2)
    one = across(block_for(z ^ 1), "dp", 1)
    mine = block_for(z)
    rows_first = gather_rows(jnp.where(outer, far, mine))

    chain = []
    work = []

    def piece_of(rows, j, arrived=None):
        out = share(index, rows, up_weight, pieces[j], arrived=arrived, deps=slot_gate[0] + tuple(work[-1:]))
        out = out if arrived is not None else [out]
        work.append(out[0])
        return out

    slot_gate = [()]

    def slot(value):
        if len(chain) >= WINDOW:
            slot_gate[0] = (chain[len(chain) - WINDOW],)
        chain.append(outward(after(value, *slot_gate[0], *work), 0))
        work.clear()
        work.append(value)
        return chain[-1]

    count = len(pieces)
    first, twos, ones, lates = {}, {}, {}, {}
    hop0, hop1, hop2 = {}, {}, {}

    def add_two(j):
        twos[j], total = piece_of(rows_two, j, arrived=hop0[0, j])
        hop1[1, j] = outward(total, 1)

    def add_one(j):
        ones[j], total = piece_of(rows_one, j, arrived=hop1[1, j])
        hop2[2, j] = outward(total, 2)

    def add_late(j):
        lates[j], total = piece_of(rows_late, j, arrived=hop0[1, j])
        hop1[2, j] = outward(total, 1)

    (first[0],) = piece_of(rows_first, 0)
    hop0[0, 0] = slot(first[0])
    rows_two = gather_rows(after(two, first[0]))
    (first[1],) = piece_of(rows_first, 1)
    hop0[0, 1] = slot(first[1])
    rows_one = gather_rows(after(one, first[1]))
    (first[2],) = piece_of(rows_first, 2)

    hop0[0, 2] = slot(first[2])
    rows_late = gather_rows(after(jnp.where(outer, mine, middle), first[2]))
    (first[3],) = piece_of(rows_first, 3)

    hop0[0, 3] = slot(first[3])
    add_two(0)
    add_two(1)

    block_tenant, owner_of = lax.optimization_barrier((block_tenant, owner_of, work[-1]))[:2]
    tenant_ids = jnp.arange(tenants, dtype=jnp.int32)
    order = jnp.stack(
        [jnp.where(outer, z ^ 3, z), z ^ 2, z ^ 1, jnp.where(outer, z, z ^ 3)]
    )
    blocks_of = block_tenant.reshape(dp_count, local_blocks)
    ids = jnp.take(blocks_of, order, axis=0).reshape(-1)
    own_ids = lax.dynamic_index_in_dim(blocks_of, z, 0, keepdims=False)
    onehot = (block_tenant[None, :] == tenant_ids[:, None]).astype(jnp.float32)
    inverse = 1.0 / jnp.sum(onehot, axis=1)
    gathered = [rows_first, rows_two, rows_one, rows_late]
    features, *parts = forward(index, ids, gathered, adapter_down)
    part_own = jnp.where(outer, parts[3], parts[0])
    part_far = jnp.where(outer, parts[0], parts[3])
    sums = [across(part_far, "dp", 3), across(parts[1], "dp", 2), across(parts[2], "dp", 1)]
    work.append(features)

    hop0[1, 0] = slot(twos[0])
    add_two(2)
    back_part = backward(after(own_ids, work[-1]), grad_out, adapter_up)
    work.append(back_part)

    hop0[1, 1] = slot(twos[1])
    add_two(3)
    sums = lax.optimization_barrier((*sums, work[-1]))[:3]
    projected = part_own + sums[0] + sums[1] + sums[2]
    projected = sum_over_tensor(projected).astype(jnp.bfloat16)
    back_mine = (SCALE * sum_over_tensor(after(back_part, work[-1]))).astype(jnp.bfloat16)

    up_terms = []
    for b in range(local_blocks):
        rows = slice(b * ROWS_BLK, (b + 1) * ROWS_BLK)
        term = SCALE * lax.dot_general(
            projected[rows], grad_out[rows], (((0,), (0,)), ((), ())), preferred_element_type=jnp.float32
        )
        up_terms.append(term.astype(jnp.bfloat16))
    work.append(back_mine)

    moved_terms = [slot(up_terms[0])]
    add_late(0)
    add_one(0)

    moved_terms.append(slot(up_terms[1]))
    add_late(1)
    add_one(1)
    owner_of = after(owner_of, work[-1])
    same_owner = owner_of[:, None] == owner_of[None, :]
    earlier = tenant_ids[None, :] < tenant_ids[:, None]
    slot_of = owner_of * OWN_MAX + jnp.sum(jnp.logical_and(same_owner, earlier), axis=1)
    own_slots = z * OWN_MAX + jnp.arange(OWN_MAX, dtype=jnp.int32)
    ownership = (slot_of[None, :] == own_slots[:, None]).astype(jnp.float32)
    own_scale = jnp.sum(ownership * inverse[None, :], axis=1)
    block_slot = jnp.sum(
        jnp.where(block_tenant[:, None] == tenant_ids[None, :], slot_of[None, :], 0), axis=1
    ).reshape(dp_count, local_blocks)

    def hits(slots, batch):
        theirs = lax.dynamic_index_in_dim(block_slot, jnp.clip(batch, 0, 3), 0, keepdims=False)
        return (slots[:, None] == theirs[None, :]).astype(jnp.float32)

    def slots_at(where):
        return where * OWN_MAX + jnp.arange(OWN_MAX, dtype=jnp.int32)

    side = jnp.where(z == 1, 1, -1)
    here = jnp.concatenate([hits(slots_at(z + 2 * side), z), hits(slots_at(z + side), z)], axis=0)
    there = jnp.concatenate([hits(slots_at(z + 2 * side), z - side), hits(slots_at(z + side), z - side)], axis=0)
    middle_hits = jnp.concatenate([here, there], axis=1)
    side2 = jnp.where(z == 2, 1, -1)
    last_hits = hits(slots_at(z + side2), z)
    final_hits = jnp.concatenate([hits(own_slots, z), hits(own_slots, z - side)], axis=1) * own_scale[:, None]

    hop0[1, 2] = slot(twos[2])
    add_one(2)

    hop0[1, 3] = slot(twos[3])
    own_terms = [term[None] for term in up_terms]
    outer_terms = [term[None] for term in moved_terms]
    totals = combine(middle_hits, own_terms + outer_terms, jnp.bfloat16)
    far_terms = outward(totals[:OWN_MAX], 1)
    near_terms = outward(totals[OWN_MAX:], 1)
    work.append(totals)
    add_one(3)

    hop0[2, 0] = slot(ones[0])
    add_late(2)

    hop0[2, 1] = slot(ones[1])
    add_late(3)
    backs = [across(after(back_mine, work[-1]), "dp", d) for d in (3, 2, 1)]

    hop0[2, 2] = slot(ones[2])
    own_mask = jnp.broadcast_to(
        (after(own_ids, work[-1])[:, None] == tenant_ids[None, :])[:, None, :, None],
        (local_blocks, ROWS_BLK, tenants, rank_width),
    )
    wide = jnp.where(
        own_mask, projected.reshape(local_blocks, ROWS_BLK, 1, rank_width), jnp.zeros((), jnp.bfloat16)
    ).reshape(batch_rows, tenants * rank_width)
    bases = []
    for j, (start, tiles) in enumerate(pieces):
        total = SCALE * jnp.dot(
            wide, flat_up[:, start * tile : (start + tiles) * tile], preferred_element_type=jnp.float32
        )
        bases.append(total + jnp.where(outer, lates[j], first[j]).astype(jnp.float32))
        work.append(bases[-1])

    hop0[2, 3] = slot(ones[3])
    far_terms = after(far_terms, work[-1])
    last_terms = outward(combine(last_hits, own_terms, jnp.bfloat16, jnp.ones((OWN_MAX,), jnp.float32), [far_terms]), 2)
    backs = [
        jnp.where(outer, backs[0], back_mine), backs[1], backs[2], jnp.where(outer, back_mine, backs[0])
    ]
    grad_down = down_gradient(ids, inverse, features, backs, adapter_down.shape)
    grad_up = combine(final_hits, own_terms + outer_terms, jnp.float32, own_scale, [near_terms, last_terms])

    layer_out = jnp.zeros((batch_rows, hidden), jnp.bfloat16)
    for j, (start, tiles) in enumerate(pieces):
        total = bases[j] + hop2[2, j].astype(jnp.float32) + hop1[2, j].astype(jnp.float32)
        total = total + hop0[2, j].astype(jnp.float32)
        layer_out = lax.dynamic_update_slice(layer_out, total.astype(jnp.bfloat16), (0, start * tile))
    return (layer_out, grad_down, grad_up)


def local_plain(tokens, up_weight, adapter_down, adapter_up, grad_out, block_tenant, owner_of):
    dp_count = lax.axis_size("dp")
    dp_index = lax.axis_index("dp")
    tp_index = lax.axis_index("tensor")
    seq_rows, feature_count = tokens.shape
    batch_rows = grad_out.shape[0]
    local_blocks = batch_rows // ROWS_BLK
    all_blocks = local_blocks * dp_count
    column_part = feature_count // dp_count
    slice_cols = adapter_down.shape[2]
    rank_width = adapter_down.shape[1]
    tenants = adapter_down.shape[0]
    gathered = lax.all_gather(tokens, "tensor", axis=0, tiled=True)
    spread = lax.all_to_all(
        gathered.reshape(1, batch_rows, dp_count, column_part),
        "dp",
        split_axis=2,
        concat_axis=0,
        tiled=True,
    )
    all_rows = spread.reshape(dp_count * batch_rows, column_part)
    base_out = lax.psum_scatter(
        jnp.dot(all_rows, up_weight, preferred_element_type=jnp.float32).astype(jnp.bfloat16),
        "dp",
        scatter_dimension=0,
        tiled=True,
    ).astype(jnp.float32)
    slice_start = tp_index * slice_cols
    feature_slice = lax.dynamic_slice_in_dim(all_rows, slice_start, slice_cols, 1).reshape(
        all_blocks, ROWS_BLK, slice_cols
    )
    down_blocks = jnp.take(adapter_down, block_tenant, axis=0)
    proj_part = jnp.einsum(
        "nrd,nkd->nrk", feature_slice, down_blocks, preferred_element_type=jnp.float32
    )
    local_ids = lax.dynamic_slice_in_dim(block_tenant, dp_index * local_blocks, local_blocks, 0)
    up_mine = jnp.take(adapter_up, local_ids, axis=0)
    out_blocks = grad_out.reshape(local_blocks, ROWS_BLK, grad_out.shape[1])
    back_part = jnp.einsum("nrf,nkf->nrk", out_blocks, up_mine, preferred_element_type=jnp.float32)
    back_full = lax.dynamic_update_slice_in_dim(
        jnp.zeros((all_blocks, ROWS_BLK, rank_width), jnp.float32),
        back_part,
        dp_index * local_blocks,
        0,
    )
    proj_sum, back_sum = lax.psum(
        (proj_part.reshape(-1, 2 * rank_width), back_full.reshape(-1, 2 * rank_width)),
        ("dp", "tensor"),
    )
    projected = proj_sum.reshape(all_blocks, ROWS_BLK, rank_width).astype(jnp.bfloat16)
    back_proj = (SCALE * back_sum).reshape(all_blocks, ROWS_BLK, rank_width).astype(jnp.bfloat16)
    proj_mine = lax.dynamic_slice_in_dim(projected, dp_index * local_blocks, local_blocks, 0)
    adapter_term = jnp.einsum(
        "nrk,nkf->nrf", proj_mine, up_mine, preferred_element_type=jnp.float32
    ).reshape(batch_rows, -1)
    layer_out = (base_out + SCALE * adapter_term).astype(jnp.bfloat16)
    down_terms = jnp.einsum(
        "nrk,nrd->nkd", back_proj, feature_slice, preferred_element_type=jnp.float32
    )
    tenant_ids = jnp.arange(tenants, dtype=jnp.int32)
    onehot = (block_tenant[None, :] == tenant_ids[:, None]).astype(jnp.float32)
    inverse = 1.0 / jnp.sum(onehot, axis=1)
    grad_down = (
        jnp.einsum("tn,nkd->tkd", onehot, down_terms, precision=lax.Precision.HIGHEST)
        * inverse[:, None, None]
    )
    up_terms = SCALE * jnp.einsum(
        "nrk,nrf->nkf", proj_mine, out_blocks, preferred_element_type=jnp.float32
    )
    same_owner = owner_of[:, None] == owner_of[None, :]
    earlier = tenant_ids[None, :] < tenant_ids[:, None]
    rank_in = jnp.sum(jnp.logical_and(same_owner, earlier), axis=1)
    slot_of = owner_of * OWN_MAX + rank_in
    own_slots = dp_index * OWN_MAX + jnp.arange(OWN_MAX, dtype=jnp.int32)
    ownership = (slot_of[None, :] == own_slots[:, None]).astype(jnp.float32)
    own_scale = jnp.dot(ownership, inverse, precision=lax.Precision.HIGHEST)
    total_slots = dp_count * OWN_MAX
    local_slots = jnp.take(slot_of, local_ids, axis=0)
    placement = (local_slots[None, :] == jnp.arange(total_slots, dtype=jnp.int32)[:, None]).astype(
        jnp.float32
    )
    buffer = jnp.einsum("sn,nkf->skf", placement, up_terms, precision=lax.Precision.HIGHEST)
    summed = lax.psum_scatter(
        buffer.astype(jnp.bfloat16), "dp", scatter_dimension=0, tiled=True
    ).astype(jnp.float32)
    grad_up = summed * own_scale[:, None, None]
    return (layer_out, grad_down, grad_up)


def solution(mesh):
    placed = (
        P(("groups", "dp", "tensor"), None),
        P("dp", "tensor"),
        P("groups", None, ("dp", "tensor")),
        P("groups", None, "tensor"),
        P(("groups", "dp"), "tensor"),
        P("groups"),
        P("groups"),
    )
    return jax.shard_map(
        local if mesh.shape["dp"] == 4 else local_plain,
        mesh=mesh,
        in_specs=placed,
        out_specs=(
            P(("groups", "dp"), "tensor"),
            P("groups", None, ("dp", "tensor")),
            P(("groups", "dp"), None, "tensor"),
        ),
        check_vma=False,
    )
```

```python
import functools

import jax
import jax.numpy as jnp
from jax import lax
from jax.experimental import pallas as pl
from jax.experimental.pallas import tpu as pltpu
from jax.sharding import PartitionSpec as P

ROWS_BLK = 128
OWN_MAX = 2
SCALE = 0.5
SPLIT = ((0, 2), (2, 5), (5, 9), (9, 13))
WINDOW = 2
VMEM = 60 * 1024 * 1024
ANY = pl.BlockSpec(memory_space=pl.ANY)
SMEM = pl.BlockSpec(memory_space=pltpu.SMEM)


class Held:
    def __init__(self, now):
        self.now = now


def tie(*held):
    distinct = list({id(one): one for one in held}.values())
    for one, now in zip(distinct, lax.optimization_barrier(tuple(one.now for one in distinct))):
        one.now = now


def after(value, *earlier):
    return lax.optimization_barrier((value, *earlier))[0]


def across(value, axis, bit):
    count = lax.axis_size(axis)
    return lax.ppermute(value, axis, [(i, i ^ bit) for i in range(count)])


def outward(value, hop):
    last = lax.axis_size("dp") - 1
    return lax.ppermute(value, "dp", [(hop, hop + 1), (last - hop, last - hop - 1)])


def bits_of(count):
    return [1 << k for k in reversed(range(count.bit_length() - 1))]


def gather_rows(rows):
    held = [(0, rows)]
    for bit in bits_of(lax.axis_size("tensor")):
        held = held + [(mask | bit, across(value, "tensor", bit)) for mask, value in held]
    return held


def sum_over_tensor(value):
    for bit in bits_of(lax.axis_size("tensor")):
        value = value + across(value, "tensor", bit)
    return value


def tile_of(width):
    return 512 if width % 512 == 0 else 128


def cut(width):
    tiles = width // tile_of(width)
    counts = [tiles * (i + 1) // 13 - tiles * i // 13 for i in range(13)]
    counts = [sum(counts[a:b]) for a, b in SPLIT]
    edges = [0]
    for n in counts:
        edges.append(edges[-1] + n)
    return list(zip(edges[:-1], counts))


def call(kernel, flops, **kwargs):
    return pl.pallas_call(
        kernel,
        compiler_params=pltpu.CompilerParams(vmem_limit_bytes=VMEM),
        cost_estimate=pl.CostEstimate(flops=flops // 6, bytes_accessed=0, transcendentals=0),
        **kwargs,
    )


def share_kernel(masks, has_add, deps, index, *refs):
    blocks, refs = refs[: len(masks)], refs[len(masks) :]
    weight, refs = refs[0], refs[1:]
    if has_add:
        arrived, refs = refs[0], refs[1:]
    out = refs[deps]
    batch = blocks[0]
    if len(masks) > 1:
        batch = refs[deps + 1]
        rows = blocks[0].shape[0]

        @pl.when(pl.program_id(0) == 0)
        def _():
            for mask, block in zip(masks, blocks):
                first = pl.multiple_of((index[0] ^ mask) * rows, rows)
                batch[pl.ds(first, rows), :] = block[...]

    value = jnp.dot(batch[...], weight[...], preferred_element_type=jnp.float32)
    if has_add:
        value = value + arrived[...].astype(jnp.float32)
    out[...] = value.astype(jnp.bfloat16)


def share(index, gathered, weight, piece, arrived=None, deps=()):
    masks, blocks = zip(*gathered)
    rows, depth = blocks[0].shape
    batch_rows = rows * len(blocks)
    tile = tile_of(weight.shape[1])
    first, count = piece
    column = pl.BlockSpec((batch_rows, tile), lambda i, s: (0, i))
    has_add = arrived is not None
    return call(
        functools.partial(share_kernel, masks, has_add, len(deps)),
        2 * batch_rows * depth * count * tile,
        out_shape=jax.ShapeDtypeStruct((batch_rows, count * tile), jnp.bfloat16),
        grid_spec=pltpu.PrefetchScalarGridSpec(
            num_scalar_prefetch=1,
            grid=(count,),
            in_specs=[pl.BlockSpec((rows, depth), lambda i, s: (0, 0))] * len(blocks)
            + [pl.BlockSpec((depth, tile), lambda i, s: (0, first + i))]
            + [column] * has_add
            + [ANY] * len(deps),
            out_specs=column,
            scratch_shapes=[pltpu.VMEM((batch_rows, depth), jnp.bfloat16)] * (len(blocks) > 1),
        ),
    )(index, *blocks, weight, *([arrived] if has_add else []), *deps)


def forward_kernel(count, deps, ids, *refs):
    blocks, down, outs = refs[:count], refs[count], refs[count + 1 + deps :]
    slices, _, _, width = down.shape
    for d in range(count):
        outs[d][...] = sum(
            lax.dot_general(
                blocks[d][:, n * width : (n + 1) * width],
                down[n, ids[d]],
                (((1,), (1,)), ((), ())),
                preferred_element_type=jnp.float32,
            )
            for n in range(slices)
        )


def forward(ids, blocks, down, deps):
    rows = blocks[0].shape[0]
    rank_width = down.shape[2]
    whole = pl.BlockSpec(memory_space=pltpu.VMEM)
    return call(
        functools.partial(forward_kernel, len(blocks), len(deps)),
        2 * len(blocks) * blocks[0].size * rank_width * 4,
        out_shape=[jax.ShapeDtypeStruct((rows, rank_width), jnp.float32)] * len(blocks),
        in_specs=[SMEM] + [whole] * (len(blocks) + 1) + [ANY] * len(deps),
        out_specs=[whole] * len(blocks),
    )(ids, *blocks, down, *deps)


def backward_kernel(ids, grad, up, out):
    @pl.when(pl.program_id(0) == 0)
    def _():
        out[...] = jnp.zeros_like(out)

    for b in range(grad.shape[0] // ROWS_BLK):
        rows = slice(b * ROWS_BLK, (b + 1) * ROWS_BLK)
        out[rows, :] += lax.dot_general(
            grad[rows, :], up[ids[b]], (((1,), (1,)), ((), ())), preferred_element_type=jnp.float32
        )


def backward(ids, grad_out, adapter_up):
    batch_rows, hidden = grad_out.shape
    tenants, rank_width, _ = adapter_up.shape
    tile = tile_of(hidden)
    return call(
        backward_kernel,
        2 * batch_rows * hidden * rank_width * 4,
        out_shape=jax.ShapeDtypeStruct((batch_rows, rank_width), jnp.float32),
        grid_spec=pltpu.PrefetchScalarGridSpec(
            num_scalar_prefetch=1,
            grid=(hidden // tile,),
            in_specs=[
                pl.BlockSpec((batch_rows, tile), lambda i, n: (0, i)),
                pl.BlockSpec((tenants, rank_width, tile), lambda i, n: (0, 0, i)),
            ],
            out_specs=pl.BlockSpec((batch_rows, rank_width), lambda i, n: (0, 0)),
        ),
    )(ids, grad_out, adapter_up)


def down_kernel(masks, index, ids, inverse, *refs):
    out = refs[-1]
    out[...] = jnp.zeros_like(out)
    at = 0
    backs, refs = refs[: len(masks)], refs[len(masks) :]
    local_blocks = backs[0].shape[0] // ROWS_BLK
    for d, parts in enumerate(masks):
        for mask in parts:
            rows = refs[at].shape[0]
            first = 0 if len(parts) == 1 else pl.multiple_of((index[0] ^ mask) * rows, rows)
            step = min(rows, ROWS_BLK)
            for k in range(0, rows, step):
                tenant = ids[d * local_blocks + (first + k) // ROWS_BLK]
                out[tenant] += lax.dot_general(
                    backs[d][pl.ds(first + k, step), :],
                    refs[at][k : k + step, :],
                    (((0,), (0,)), ((), ())),
                    preferred_element_type=jnp.float32,
                )
            at += 1
    for n in range(out.shape[0]):
        out[n] *= inverse[n]


def down_gradient(index, ids, inverse, gathered, backs, shape):
    masks = [[mask for mask, _ in parts] for parts in gathered]
    arrays = [value for parts in gathered for _, value in parts]
    slice_cols = shape[2]
    return call(
        functools.partial(down_kernel, masks),
        8 * shape[1] * slice_cols * sum(value.shape[0] for value in arrays),
        out_shape=jax.ShapeDtypeStruct(shape, jnp.float32),
        grid_spec=pltpu.PrefetchScalarGridSpec(
            num_scalar_prefetch=2,
            grid=(1,),
            in_specs=[SMEM]
            + [pl.BlockSpec(back.shape, lambda i, s, n: (0, 0)) for back in backs]
            + [pl.BlockSpec((value.shape[0], slice_cols), lambda i, s, n: (0, s[0])) for value in arrays],
            out_specs=pl.BlockSpec(shape, lambda i, s, n: (0, 0, 0)),
        ),
    )(index, ids, inverse, *backs, *arrays)


def combine_kernel(count, extras, weights, scale, *refs):
    terms, more, out = refs[:count], refs[count : count + extras], refs[count + extras]
    parts = [term[0].astype(jnp.float32) for term in terms]
    for s in range(out.shape[0]):
        total = sum(part * weights[s, n] for n, part in enumerate(parts))
        if extras:
            total += sum(extra[s].astype(jnp.float32) for extra in more) * scale[s]
        out[s] = total.astype(out.dtype)


def combine(weights, terms, dtype, scale=None, extras=()):
    rank_width, hidden = terms[0].shape[1:]
    tile = tile_of(hidden)
    slots = weights.shape[0]
    if scale is None:
        scale = jnp.ones((slots,), jnp.float32)
    return call(
        functools.partial(combine_kernel, len(terms), len(extras)),
        4 * slots * rank_width * hidden * len(terms),
        out_shape=jax.ShapeDtypeStruct((slots, rank_width, hidden), dtype),
        grid=(hidden // tile,),
        in_specs=[SMEM, SMEM]
        + [pl.BlockSpec((1, rank_width, tile), lambda i: (0, 0, i))] * len(terms)
        + [pl.BlockSpec((slots, rank_width, tile), lambda i: (0, 0, i))] * len(extras),
        out_specs=pl.BlockSpec((slots, rank_width, tile), lambda i: (0, 0, i)),
    )(weights, scale, *terms, *extras)


def local(tokens, up_weight, adapter_down, adapter_up, grad_out, block_tenant, owner_of):
    dp_count = 4
    z = lax.axis_index("dp")
    t = lax.axis_index("tensor")
    outer = jnp.logical_or(z == 0, z == 3)
    part_rows, feature_count = tokens.shape
    batch_rows, hidden = grad_out.shape
    local_blocks = batch_rows // ROWS_BLK
    depth = feature_count // dp_count
    tenants, rank_width, slice_cols = adapter_down.shape
    flat_up = adapter_up.reshape(tenants * rank_width, hidden)
    pieces = cut(hidden)
    tile = tile_of(hidden)
    index = t.reshape(1)

    def block_for(where):
        return lax.dynamic_slice_in_dim(tokens, where * depth, depth, 1)

    def first_hop(value):
        return lax.ppermute(value, "dp", [(0, 1), (3, 2)])

    def middle_hop(value):
        return lax.ppermute(value, "dp", [(1, 2), (2, 1)])

    def last_hop(value):
        return lax.ppermute(value, "dp", [(1, 0), (2, 3)])

    def first_and_last_hop(value):
        return lax.ppermute(value, "dp", [(0, 1), (3, 2), (1, 0), (2, 3)])

    def gather(value):
        return [(0, lax.all_gather(value, "tensor", axis=0, tiled=True))]

    down_all = lax.all_gather(adapter_down, "tensor", axis=0)
    far = lax.ppermute(block_for(z ^ 3), "dp", [(0, 3), (3, 0)])
    two = across(block_for(z ^ 2), "dp", 2)
    one = across(block_for(z ^ 1), "dp", 1)
    far, two, one = lax.optimization_barrier((far, two, one))
    middle = middle_hop(after(block_for(z ^ 3), far))
    mine = block_for(z)
    first_part = jnp.where(outer, far, mine)
    rows_first = gather_rows(first_part)

    chain = []
    work, earlier_work, pinned = [], [], []
    slot_gate = []

    def slot(value, hop=first_hop):
        k = len(chain)
        slot_gate[:] = chain[max(k - WINDOW, 0) : max(k - WINDOW + 1, 0)]
        with jax.named_scope(f"send{k}"):
            tie(value, *slot_gate, *pinned, *earlier_work)
            chain.append(Held(hop(value.now)))
        earlier_work[:] = work[-1:]
        pinned.clear()
        return chain[-1]

    def pin(arrived):
        pinned.append(arrived)

    def do(value):
        work.append(Held(value))
        return work[-1]

    def late_use(value):
        held = Held(value)
        tie(held, *work[-1:])
        return held.now

    def piece_of(name, rows, j, arrived=None):
        arrived = arrived if arrived is None else arrived.now
        deps = [held.now for held in (*slot_gate, *work[-1:])]
        with jax.named_scope(f"{name}{j}"):
            return do(share(index, rows, up_weight, pieces[j], arrived=arrived, deps=deps))

    firsts, twos, ones, lates = {}, {}, {}, {}
    step0, step1, step2, mid1, mid2 = {}, {}, {}, {}, {}

    def add_two(j):
        twos[j] = piece_of("two", rows_two, j, step0[j])
        with jax.named_scope(f"mid_two{j}"):
            mid1[j] = Held(middle_hop(twos[j].now))

    def add_late(j):
        lates[j] = piece_of("late", rows_late, j, step1[j])
        with jax.named_scope(f"mid_late{j}"):
            mid2[j] = Held(middle_hop(lates[j].now))

    def add_one(j):
        ones[j] = piece_of("one", rows_one, j, mid1[j])

    firsts[0] = piece_of("first", rows_first, 0)
    with jax.named_scope("two_rows"):
        two = late_use(two)
        rows_two = gather(two)

    step0[0] = slot(firsts[0])
    firsts[1] = piece_of("first", rows_first, 1)
    with jax.named_scope("one_rows"):
        one = late_use(one)
        rows_one = gather(one)
    with jax.named_scope("late_rows"):
        late_part = jnp.where(outer, mine, late_use(middle))
        rows_late = gather(late_part)
    block_tenant = late_use(block_tenant)

    step0[1] = slot(firsts[1])
    firsts[2] = piece_of("first", rows_first, 2)

    tenant_ids = jnp.arange(tenants, dtype=jnp.int32)
    order = jnp.stack([jnp.where(outer, z ^ 3, z), z ^ 2, z ^ 1, jnp.where(outer, z, z ^ 3)])
    blocks_of = block_tenant.reshape(dp_count, local_blocks)
    ids = jnp.take(blocks_of, order, axis=0)
    row_ids = lax.dynamic_index_in_dim(ids, t * part_rows // ROWS_BLK, 1, keepdims=False)
    ids = ids.reshape(-1)
    own_ids = lax.dynamic_index_in_dim(blocks_of, z, 0, keepdims=False)
    with jax.named_scope("forward"):
        parts = jnp.stack(forward(row_ids, [first_part, two, one, late_part], down_all, (firsts[2].now,)))
        by_batch = jnp.where((order[None, :] == jnp.arange(dp_count)[:, None])[:, :, None, None], parts, 0.0)
        by_batch = do(jnp.sum(by_batch, axis=1)).now
        projected = lax.psum_scatter(by_batch, "dp", scatter_dimension=0, tiled=True)[0]

    step0[2] = slot(firsts[2])
    firsts[3] = piece_of("first", rows_first, 3)
    add_two(0)

    step0[3] = slot(firsts[3])
    with jax.named_scope("projected"):
        projected = late_use(projected).astype(jnp.bfloat16)
        projected = lax.all_gather(projected, "tensor", axis=0, tiled=True)
    add_two(1)
    projected = late_use(projected)
    up_terms = []
    for b in range(local_blocks):
        rows = slice(b * ROWS_BLK, (b + 1) * ROWS_BLK)
        term = SCALE * lax.dot_general(
            projected[rows], grad_out[rows], (((0,), (0,)), ((), ())), preferred_element_type=jnp.float32
        )
        up_terms.append(do(term.astype(jnp.bfloat16)))

    moved_terms = [slot(up_terms[0])]
    add_two(2)
    pin(mid1[0])

    moved_terms.append(slot(up_terms[1]))
    add_two(3)
    pin(mid1[1])
    owner_of = late_use(owner_of)
    onehot = (block_tenant[None, :] == tenant_ids[:, None]).astype(jnp.float32)
    inverse = 1.0 / jnp.sum(onehot, axis=1)
    same_owner = owner_of[:, None] == owner_of[None, :]
    earlier = tenant_ids[None, :] < tenant_ids[:, None]
    slot_of = owner_of * OWN_MAX + jnp.sum(jnp.logical_and(same_owner, earlier), axis=1)
    own_slots = z * OWN_MAX + jnp.arange(OWN_MAX, dtype=jnp.int32)
    ownership = (slot_of[None, :] == own_slots[:, None]).astype(jnp.float32)
    own_scale = jnp.sum(ownership * inverse[None, :], axis=1)
    block_slot = jnp.sum(
        jnp.where(block_tenant[:, None] == tenant_ids[None, :], slot_of[None, :], 0), axis=1
    ).reshape(dp_count, local_blocks)

    def hits(slots, batch):
        theirs = lax.dynamic_index_in_dim(block_slot, jnp.clip(batch, 0, 3), 0, keepdims=False)
        return (slots[:, None] == theirs[None, :]).astype(jnp.float32)

    def slots_at(where):
        return where * OWN_MAX + jnp.arange(OWN_MAX, dtype=jnp.int32)

    side = jnp.where(z == 1, 1, -1)
    far_hits = jnp.concatenate([hits(slots_at(z + 2 * side), z), hits(slots_at(z + 2 * side), z - side)], axis=1)
    near_hits = jnp.concatenate([hits(slots_at(z + side), z), hits(slots_at(z + side), z - side)], axis=1)
    last_hits = hits(slots_at(jnp.where(z == 2, 3, 0)), z)
    own_hits = jnp.concatenate([hits(own_slots, z), hits(own_slots, z - side)], axis=1) * own_scale[:, None]

    add_one(0)

    step1[0] = slot(twos[0])
    pin(mid1[2])
    add_one(1)
    back_part = do(backward(late_use(own_ids), grad_out, adapter_up))
    with jax.named_scope("back_mine"):
        back_mine = (SCALE * lax.psum(back_part.now, "tensor")).astype(jnp.bfloat16)

    step1[1] = slot(twos[1])

    def terms():
        return [held.now[None] for held in (*up_terms, *moved_terms)]

    with jax.named_scope("far_terms"):
        far_sums = do(combine(far_hits, terms(), jnp.bfloat16))
        far_terms = Held(middle_hop(far_sums.now))
    pin(mid1[3])
    with jax.named_scope("backs"):
        backs = lax.all_gather(late_use(back_mine), "dp", axis=0)

    step2[0] = slot(ones[0], first_and_last_hop)
    add_late(0)
    add_one(2)

    step2[1] = slot(ones[1], first_and_last_hop)
    add_late(1)
    pin(far_terms)
    with jax.named_scope("last_terms"):
        last_sums = do(
            combine(last_hits, terms()[:local_blocks], jnp.bfloat16, jnp.ones((OWN_MAX,), jnp.float32), [far_terms.now])
        )
        last_terms = Held(last_hop(last_sums.now))

    step1[2] = slot(twos[2])
    with jax.named_scope("near_terms"):
        near_sums = do(combine(near_hits, terms(), jnp.bfloat16))
        near_terms = Held(middle_hop(near_sums.now))
    pin(mid2[0])
    add_one(3)

    step1[3] = slot(twos[3])
    pin(mid2[1])
    backs = late_use(backs)
    backs = [lax.dynamic_index_in_dim(backs, order[n], 0, keepdims=False) for n in range(dp_count)]
    grad_down = do(
        down_gradient(
            index, ids, inverse, [rows_first, rows_two, rows_one, rows_late], backs, adapter_down.shape
        )
    )
    pin(last_terms)

    step2[2] = slot(ones[2], first_and_last_hop)
    add_late(2)
    pin(near_terms)

    step2[3] = slot(ones[3], first_and_last_hop)
    add_late(3)
    grad_up = combine(own_hits, terms(), jnp.float32, own_scale, [near_terms.now, last_terms.now])
    own_mask = jnp.broadcast_to(
        (late_use(own_ids)[:, None] == tenant_ids[None, :])[:, None, :, None],
        (local_blocks, ROWS_BLK, tenants, rank_width),
    )
    wide = jnp.where(
        own_mask, projected.reshape(local_blocks, ROWS_BLK, 1, rank_width), jnp.zeros((), jnp.bfloat16)
    ).reshape(batch_rows, tenants * rank_width)
    layer_out = jnp.zeros((batch_rows, hidden), jnp.bfloat16)
    for j, (start, tiles) in enumerate(pieces):
        total = SCALE * jnp.dot(
            wide, flat_up[:, start * tile : (start + tiles) * tile], preferred_element_type=jnp.float32
        )
        total = total + jnp.where(outer, lates[j].now, firsts[j].now).astype(jnp.float32)
        total = total + mid2[j].now.astype(jnp.float32)
        total = total + step2[j].now.astype(jnp.float32)
        layer_out = lax.dynamic_update_slice(layer_out, total.astype(jnp.bfloat16), (0, start * tile))
    return (layer_out, grad_down.now, grad_up)


def local_plain(tokens, up_weight, adapter_down, adapter_up, grad_out, block_tenant, owner_of):
    dp_count = lax.axis_size("dp")
    dp_index = lax.axis_index("dp")
    tp_index = lax.axis_index("tensor")
    seq_rows, feature_count = tokens.shape
    batch_rows = grad_out.shape[0]
    local_blocks = batch_rows // ROWS_BLK
    all_blocks = local_blocks * dp_count
    column_part = feature_count // dp_count
    slice_cols = adapter_down.shape[2]
    rank_width = adapter_down.shape[1]
    tenants = adapter_down.shape[0]
    gathered = lax.all_gather(tokens, "tensor", axis=0, tiled=True)
    spread = lax.all_to_all(
        gathered.reshape(1, batch_rows, dp_count, column_part),
        "dp",
        split_axis=2,
        concat_axis=0,
        tiled=True,
    )
    all_rows = spread.reshape(dp_count * batch_rows, column_part)
    base_out = lax.psum_scatter(
        jnp.dot(all_rows, up_weight, preferred_element_type=jnp.float32).astype(jnp.bfloat16),
        "dp",
        scatter_dimension=0,
        tiled=True,
    ).astype(jnp.float32)
    slice_start = tp_index * slice_cols
    feature_slice = lax.dynamic_slice_in_dim(all_rows, slice_start, slice_cols, 1).reshape(
        all_blocks, ROWS_BLK, slice_cols
    )
    down_blocks = jnp.take(adapter_down, block_tenant, axis=0)
    proj_part = jnp.einsum(
        "nrd,nkd->nrk", feature_slice, down_blocks, preferred_element_type=jnp.float32
    )
    local_ids = lax.dynamic_slice_in_dim(block_tenant, dp_index * local_blocks, local_blocks, 0)
    up_mine = jnp.take(adapter_up, local_ids, axis=0)
    out_blocks = grad_out.reshape(local_blocks, ROWS_BLK, grad_out.shape[1])
    back_part = jnp.einsum("nrf,nkf->nrk", out_blocks, up_mine, preferred_element_type=jnp.float32)
    back_full = lax.dynamic_update_slice_in_dim(
        jnp.zeros((all_blocks, ROWS_BLK, rank_width), jnp.float32),
        back_part,
        dp_index * local_blocks,
        0,
    )
    proj_sum, back_sum = lax.psum(
        (proj_part.reshape(-1, 2 * rank_width), back_full.reshape(-1, 2 * rank_width)),
        ("dp", "tensor"),
    )
    projected = proj_sum.reshape(all_blocks, ROWS_BLK, rank_width).astype(jnp.bfloat16)
    back_proj = (SCALE * back_sum).reshape(all_blocks, ROWS_BLK, rank_width).astype(jnp.bfloat16)
    proj_mine = lax.dynamic_slice_in_dim(projected, dp_index * local_blocks, local_blocks, 0)
    adapter_term = jnp.einsum(
        "nrk,nkf->nrf", proj_mine, up_mine, preferred_element_type=jnp.float32
    ).reshape(batch_rows, -1)
    layer_out = (base_out + SCALE * adapter_term).astype(jnp.bfloat16)
    down_terms = jnp.einsum(
        "nrk,nrd->nkd", back_proj, feature_slice, preferred_element_type=jnp.float32
    )
    tenant_ids = jnp.arange(tenants, dtype=jnp.int32)
    onehot = (block_tenant[None, :] == tenant_ids[:, None]).astype(jnp.float32)
    inverse = 1.0 / jnp.sum(onehot, axis=1)
    grad_down = (
        jnp.einsum("tn,nkd->tkd", onehot, down_terms, precision=lax.Precision.HIGHEST)
        * inverse[:, None, None]
    )
    up_terms = SCALE * jnp.einsum(
        "nrk,nrf->nkf", proj_mine, out_blocks, preferred_element_type=jnp.float32
    )
    same_owner = owner_of[:, None] == owner_of[None, :]
    earlier = tenant_ids[None, :] < tenant_ids[:, None]
    rank_in = jnp.sum(jnp.logical_and(same_owner, earlier), axis=1)
    slot_of = owner_of * OWN_MAX + rank_in
    own_slots = dp_index * OWN_MAX + jnp.arange(OWN_MAX, dtype=jnp.int32)
    ownership = (slot_of[None, :] == own_slots[:, None]).astype(jnp.float32)
    own_scale = jnp.dot(ownership, inverse, precision=lax.Precision.HIGHEST)
    total_slots = dp_count * OWN_MAX
    local_slots = jnp.take(slot_of, local_ids, axis=0)
    placement = (local_slots[None, :] == jnp.arange(total_slots, dtype=jnp.int32)[:, None]).astype(
        jnp.float32
    )
    buffer = jnp.einsum("sn,nkf->skf", placement, up_terms, precision=lax.Precision.HIGHEST)
    summed = lax.psum_scatter(
        buffer.astype(jnp.bfloat16), "dp", scatter_dimension=0, tiled=True
    ).astype(jnp.float32)
    grad_up = summed * own_scale[:, None, None]
    return (layer_out, grad_down, grad_up)


def solution(mesh):
    placed = (
        P(("groups", "dp", "tensor"), None),
        P("dp", "tensor"),
        P("groups", None, ("dp", "tensor")),
        P("groups", None, "tensor"),
        P(("groups", "dp"), "tensor"),
        P("groups"),
        P("groups"),
    )
    return jax.shard_map(
        local if mesh.shape["dp"] == 4 else local_plain,
        mesh=mesh,
        in_specs=placed,
        out_specs=(
            P(("groups", "dp"), "tensor"),
            P("groups", None, ("dp", "tensor")),
            P(("groups", "dp"), None, "tensor"),
        ),
        check_vma=False,
    )
```

```python
import functools

import jax
import jax.numpy as jnp
from jax import lax
from jax.experimental import pallas as pl
from jax.experimental.pallas import tpu as pltpu
from jax.sharding import PartitionSpec as P

ROWS_BLK = 128
OWN_MAX = 2
SCALE = 0.5
SPLIT = ((0, 2), (2, 5), (5, 9), (9, 13))
WINDOW = 2
VMEM = 60 * 1024 * 1024
ANY = pl.BlockSpec(memory_space=pl.ANY)
SMEM = pl.BlockSpec(memory_space=pltpu.SMEM)


class Held:
    def __init__(self, now):
        self.now = now


def tie(*held):
    distinct = list({id(one): one for one in held}.values())
    for one, now in zip(distinct, lax.optimization_barrier(tuple(one.now for one in distinct))):
        one.now = now


def after(value, *earlier):
    return lax.optimization_barrier((value, *earlier))[0]


def across(value, axis, bit):
    count = lax.axis_size(axis)
    return lax.ppermute(value, axis, [(i, i ^ bit) for i in range(count)])


def outward(value, hop):
    last = lax.axis_size("dp") - 1
    return lax.ppermute(value, "dp", [(hop, hop + 1), (last - hop, last - hop - 1)])


def bits_of(count):
    return [1 << k for k in reversed(range(count.bit_length() - 1))]


def gather_rows(rows):
    held = [(0, rows)]
    for bit in bits_of(lax.axis_size("tensor")):
        held = held + [(mask | bit, across(value, "tensor", bit)) for mask, value in held]
    return held


def sum_over_tensor(value):
    for bit in bits_of(lax.axis_size("tensor")):
        value = value + across(value, "tensor", bit)
    return value


def tile_of(width):
    return 512 if width % 512 == 0 else 128


def cut(width):
    tiles = width // tile_of(width)
    counts = [tiles * (i + 1) // 13 - tiles * i // 13 for i in range(13)]
    counts = [sum(counts[a:b]) for a, b in SPLIT]
    edges = [0]
    for n in counts:
        edges.append(edges[-1] + n)
    return list(zip(edges[:-1], counts))


def call(kernel, flops, **kwargs):
    return pl.pallas_call(
        kernel,
        compiler_params=pltpu.CompilerParams(vmem_limit_bytes=VMEM),
        cost_estimate=pl.CostEstimate(flops=10 * flops, bytes_accessed=0, transcendentals=0),
        **kwargs,
    )


def share_kernel(masks, has_add, deps, index, *refs):
    blocks, refs = refs[: len(masks)], refs[len(masks) :]
    weight, refs = refs[0], refs[1:]
    if has_add:
        arrived, refs = refs[0], refs[1:]
    out = refs[deps]
    batch = blocks[0]
    if len(masks) > 1:
        batch = refs[deps + 1]
        rows = blocks[0].shape[0]

        @pl.when(pl.program_id(0) == 0)
        def _():
            for mask, block in zip(masks, blocks):
                first = pl.multiple_of((index[0] ^ mask) * rows, rows)
                batch[pl.ds(first, rows), :] = block[...]

    value = jnp.dot(batch[...], weight[...], preferred_element_type=jnp.float32)
    if has_add:
        value = value + arrived[...].astype(jnp.float32)
    out[...] = value.astype(jnp.bfloat16)


def share(index, gathered, weight, piece, arrived=None, deps=()):
    masks, blocks = zip(*gathered)
    rows, depth = blocks[0].shape
    batch_rows = rows * len(blocks)
    tile = tile_of(weight.shape[1])
    first, count = piece
    column = pl.BlockSpec((batch_rows, tile), lambda i, s: (0, i))
    has_add = arrived is not None
    return call(
        functools.partial(share_kernel, masks, has_add, len(deps)),
        2 * batch_rows * depth * count * tile,
        out_shape=jax.ShapeDtypeStruct((batch_rows, count * tile), jnp.bfloat16),
        grid_spec=pltpu.PrefetchScalarGridSpec(
            num_scalar_prefetch=1,
            grid=(count,),
            in_specs=[pl.BlockSpec((rows, depth), lambda i, s: (0, 0))] * len(blocks)
            + [pl.BlockSpec((depth, tile), lambda i, s: (0, first + i))]
            + [column] * has_add
            + [ANY] * len(deps),
            out_specs=column,
            scratch_shapes=[pltpu.VMEM((batch_rows, depth), jnp.bfloat16)] * (len(blocks) > 1),
        ),
    )(index, *blocks, weight, *([arrived] if has_add else []), *deps)


def forward_kernel(count, deps, ids, *refs):
    blocks, down, outs = refs[:count], refs[count], refs[count + 1 + deps :]
    slices, _, _, width = down.shape
    for d in range(count):
        outs[d][...] = sum(
            lax.dot_general(
                blocks[d][:, n * width : (n + 1) * width],
                down[n, ids[d]],
                (((1,), (1,)), ((), ())),
                preferred_element_type=jnp.float32,
            )
            for n in range(slices)
        )


def forward(ids, blocks, down, deps):
    rows = blocks[0].shape[0]
    rank_width = down.shape[2]
    whole = pl.BlockSpec(memory_space=pltpu.VMEM)
    return call(
        functools.partial(forward_kernel, len(blocks), len(deps)),
        2 * len(blocks) * blocks[0].size * rank_width * 4,
        out_shape=[jax.ShapeDtypeStruct((rows, rank_width), jnp.float32)] * len(blocks),
        in_specs=[SMEM] + [whole] * (len(blocks) + 1) + [ANY] * len(deps),
        out_specs=[whole] * len(blocks),
    )(ids, *blocks, down, *deps)


def backward_kernel(ids, grad, up, out):
    @pl.when(pl.program_id(0) == 0)
    def _():
        out[...] = jnp.zeros_like(out)

    for b in range(grad.shape[0] // ROWS_BLK):
        rows = slice(b * ROWS_BLK, (b + 1) * ROWS_BLK)
        out[rows, :] += lax.dot_general(
            grad[rows, :], up[ids[b]], (((1,), (1,)), ((), ())), preferred_element_type=jnp.float32
        )


def backward(ids, grad_out, adapter_up):
    batch_rows, hidden = grad_out.shape
    tenants, rank_width, _ = adapter_up.shape
    tile = hidden // 4
    return call(
        backward_kernel,
        2 * batch_rows * hidden * rank_width * 4,
        out_shape=jax.ShapeDtypeStruct((batch_rows, rank_width), jnp.float32),
        grid_spec=pltpu.PrefetchScalarGridSpec(
            num_scalar_prefetch=1,
            grid=(hidden // tile,),
            in_specs=[
                pl.BlockSpec((batch_rows, tile), lambda i, n: (0, i)),
                pl.BlockSpec((tenants, rank_width, tile), lambda i, n: (0, 0, i)),
            ],
            out_specs=pl.BlockSpec((batch_rows, rank_width), lambda i, n: (0, 0)),
        ),
    )(ids, grad_out, adapter_up)


def down_kernel(masks, index, ids, inverse, *refs):
    out = refs[-1]
    out[...] = jnp.zeros_like(out)
    at = 0
    backs, refs = refs[: len(masks)], refs[len(masks) :]
    local_blocks = backs[0].shape[0] // ROWS_BLK
    for d, parts in enumerate(masks):
        for mask in parts:
            rows = refs[at].shape[0]
            first = 0 if len(parts) == 1 else pl.multiple_of((index[0] ^ mask) * rows, rows)
            step = min(rows, ROWS_BLK)
            for k in range(0, rows, step):
                tenant = ids[d * local_blocks + (first + k) // ROWS_BLK]
                out[tenant] += lax.dot_general(
                    backs[d][pl.ds(first + k, step), :],
                    refs[at][k : k + step, :],
                    (((0,), (0,)), ((), ())),
                    preferred_element_type=jnp.float32,
                )
            at += 1
    for n in range(out.shape[0]):
        out[n] *= inverse[n]


def down_gradient(index, ids, inverse, gathered, backs, shape):
    masks = [[mask for mask, _ in parts] for parts in gathered]
    arrays = [value for parts in gathered for _, value in parts]
    slice_cols = shape[2]
    return call(
        functools.partial(down_kernel, masks),
        8 * shape[1] * slice_cols * sum(value.shape[0] for value in arrays),
        out_shape=jax.ShapeDtypeStruct(shape, jnp.float32),
        grid_spec=pltpu.PrefetchScalarGridSpec(
            num_scalar_prefetch=2,
            grid=(1,),
            in_specs=[SMEM]
            + [pl.BlockSpec(back.shape, lambda i, s, n: (0, 0)) for back in backs]
            + [pl.BlockSpec((value.shape[0], slice_cols), lambda i, s, n: (0, s[0])) for value in arrays],
            out_specs=pl.BlockSpec(shape, lambda i, s, n: (0, 0, 0)),
        ),
    )(index, ids, inverse, *backs, *arrays)


def combine_kernel(count, extras, weights, scale, *refs):
    terms, more, out = refs[:count], refs[count : count + extras], refs[count + extras]
    parts = [term[0].astype(jnp.float32) for term in terms]
    for s in range(out.shape[0]):
        total = sum(part * weights[s, n] for n, part in enumerate(parts))
        if extras:
            total += sum(extra[s].astype(jnp.float32) for extra in more) * scale[s]
        out[s] = total.astype(out.dtype)


def combine(weights, terms, dtype, scale=None, extras=()):
    rank_width, hidden = terms[0].shape[1:]
    tile = hidden // 4
    slots = weights.shape[0]
    if scale is None:
        scale = jnp.ones((slots,), jnp.float32)
    return call(
        functools.partial(combine_kernel, len(terms), len(extras)),
        4 * slots * rank_width * hidden * len(terms),
        out_shape=jax.ShapeDtypeStruct((slots, rank_width, hidden), dtype),
        grid=(hidden // tile,),
        in_specs=[SMEM, SMEM]
        + [pl.BlockSpec((1, rank_width, tile), lambda i: (0, 0, i))] * len(terms)
        + [pl.BlockSpec((slots, rank_width, tile), lambda i: (0, 0, i))] * len(extras),
        out_specs=pl.BlockSpec((slots, rank_width, tile), lambda i: (0, 0, i)),
    )(weights, scale, *terms, *extras)


def local(tokens, up_weight, adapter_down, adapter_up, grad_out, block_tenant, owner_of):
    dp_count = 4
    z = lax.axis_index("dp")
    t = lax.axis_index("tensor")
    outer = jnp.logical_or(z == 0, z == 3)
    part_rows, feature_count = tokens.shape
    batch_rows, hidden = grad_out.shape
    local_blocks = batch_rows // ROWS_BLK
    depth = feature_count // dp_count
    tenants, rank_width, slice_cols = adapter_down.shape
    flat_up = adapter_up.reshape(tenants * rank_width, hidden)
    pieces = cut(hidden)
    tile = tile_of(hidden)
    index = t.reshape(1)

    def block_for(where):
        return lax.dynamic_slice_in_dim(tokens, where * depth, depth, 1)

    def first_hop(value):
        return lax.ppermute(value, "dp", [(0, 1), (3, 2)])

    def middle_hop(value):
        return lax.ppermute(value, "dp", [(1, 2), (2, 1)])

    def last_hop(value):
        return lax.ppermute(value, "dp", [(1, 0), (2, 3)])

    def first_and_last_hop(value):
        return lax.ppermute(value, "dp", [(0, 1), (3, 2), (1, 0), (2, 3)])

    def gather(value):
        return [(0, lax.all_gather(value, "tensor", axis=0, tiled=True))]

    down_all = lax.all_gather(adapter_down, "tensor", axis=0)
    far = lax.ppermute(block_for(z ^ 3), "dp", [(0, 3), (3, 0)])
    two = across(block_for(z ^ 2), "dp", 2)
    one = across(block_for(z ^ 1), "dp", 1)
    far, two, one = lax.optimization_barrier((far, two, one))
    middle = middle_hop(after(block_for(z ^ 3), far))
    mine = block_for(z)
    first_part = jnp.where(outer, far, mine)
    rows_first = gather_rows(first_part)

    chain = []
    work, earlier_work, pinned = [], [], []
    slot_gate = []

    def slot(value, hop=first_hop):
        k = len(chain)
        slot_gate[:] = chain[max(k - WINDOW, 0) : max(k - WINDOW + 1, 0)]
        with jax.named_scope(f"send{k}"):
            tie(value, *slot_gate, *pinned, *earlier_work)
            chain.append(Held(hop(value.now)))
        earlier_work[:] = work[-1:]
        pinned.clear()
        return chain[-1]

    def pin(arrived):
        pinned.append(arrived)

    def do(value):
        work.append(Held(value))
        return work[-1]

    def late_use(value):
        held = Held(value)
        tie(held, *slot_gate, *work[-1:])
        return held.now

    def piece_of(name, rows, j, arrived=None):
        arrived = arrived if arrived is None else arrived.now
        deps = [held.now for held in (*slot_gate, *work[-1:])]
        with jax.named_scope(f"{name}{j}"):
            return do(share(index, rows, up_weight, pieces[j], arrived=arrived, deps=deps))

    firsts, twos, ones, lates = {}, {}, {}, {}
    step0, step1, step2, mid1, mid2 = {}, {}, {}, {}, {}

    def add_two(j):
        twos[j] = piece_of("two", rows_two, j, step0[j])
        with jax.named_scope(f"mid_two{j}"):
            mid1[j] = Held(middle_hop(twos[j].now))

    def add_late(j):
        lates[j] = piece_of("late", rows_late, j, step1[j])
        with jax.named_scope(f"mid_late{j}"):
            mid2[j] = Held(middle_hop(lates[j].now))

    def add_one(j):
        ones[j] = piece_of("one", rows_one, j, mid1[j])

    firsts[0] = piece_of("first", rows_first, 0)
    with jax.named_scope("two_rows"):
        two = late_use(two)
        rows_two = gather(two)

    step0[0] = slot(firsts[0])
    firsts[1] = piece_of("first", rows_first, 1)
    with jax.named_scope("one_rows"):
        one = late_use(one)
        rows_one = gather(one)
    with jax.named_scope("late_rows"):
        late_part = jnp.where(outer, mine, late_use(middle))
        rows_late = gather(late_part)
    block_tenant = late_use(block_tenant)

    step0[1] = slot(firsts[1])
    slot_gate[:] = chain[:1]
    firsts[2] = piece_of("first", rows_first, 2)

    slot_gate[:] = chain[1:2]
    tenant_ids = jnp.arange(tenants, dtype=jnp.int32)
    order = jnp.stack([jnp.where(outer, z ^ 3, z), z ^ 2, z ^ 1, jnp.where(outer, z, z ^ 3)])
    blocks_of = block_tenant.reshape(dp_count, local_blocks)
    ids = jnp.take(blocks_of, order, axis=0)
    row_ids = lax.dynamic_index_in_dim(ids, t * part_rows // ROWS_BLK, 1, keepdims=False)
    ids = ids.reshape(-1)
    own_ids = lax.dynamic_index_in_dim(blocks_of, z, 0, keepdims=False)
    with jax.named_scope("forward"):
        parts = jnp.stack(forward(late_use(row_ids), [first_part, two, one, late_part], down_all, ()))
        by_batch = jnp.where((order[None, :] == jnp.arange(dp_count)[:, None])[:, :, None, None], parts, 0.0)
        by_batch = do(jnp.sum(by_batch, axis=1)).now
        projected = lax.psum_scatter(by_batch, "dp", scatter_dimension=0, tiled=True)[0]

    step0[2] = slot(firsts[2])
    firsts[3] = piece_of("first", rows_first, 3)
    add_two(0)

    step0[3] = slot(firsts[3])
    with jax.named_scope("projected"):
        projected = late_use(projected).astype(jnp.bfloat16)
        projected = lax.all_gather(projected, "tensor", axis=0, tiled=True)
    add_two(1)
    projected = late_use(projected)
    up_terms = []
    for b in range(local_blocks):
        rows = slice(b * ROWS_BLK, (b + 1) * ROWS_BLK)
        term = SCALE * lax.dot_general(
            projected[rows], grad_out[rows], (((0,), (0,)), ((), ())), preferred_element_type=jnp.float32
        )
        up_terms.append(do(term.astype(jnp.bfloat16)))

    moved_terms = [slot(up_terms[0])]
    add_two(2)
    pin(mid1[0])

    moved_terms.append(slot(up_terms[1]))
    add_two(3)
    pin(mid1[1])
    owner_of = late_use(owner_of)
    onehot = (block_tenant[None, :] == tenant_ids[:, None]).astype(jnp.float32)
    inverse = 1.0 / jnp.sum(onehot, axis=1)
    same_owner = owner_of[:, None] == owner_of[None, :]
    earlier = tenant_ids[None, :] < tenant_ids[:, None]
    slot_of = owner_of * OWN_MAX + jnp.sum(jnp.logical_and(same_owner, earlier), axis=1)
    own_slots = z * OWN_MAX + jnp.arange(OWN_MAX, dtype=jnp.int32)
    ownership = (slot_of[None, :] == own_slots[:, None]).astype(jnp.float32)
    own_scale = jnp.sum(ownership * inverse[None, :], axis=1)
    block_slot = jnp.sum(
        jnp.where(block_tenant[:, None] == tenant_ids[None, :], slot_of[None, :], 0), axis=1
    ).reshape(dp_count, local_blocks)

    def hits(slots, batch):
        theirs = lax.dynamic_index_in_dim(block_slot, jnp.clip(batch, 0, 3), 0, keepdims=False)
        return (slots[:, None] == theirs[None, :]).astype(jnp.float32)

    def slots_at(where):
        return where * OWN_MAX + jnp.arange(OWN_MAX, dtype=jnp.int32)

    side = jnp.where(z == 1, 1, -1)
    far_hits = jnp.concatenate([hits(slots_at(z + 2 * side), z), hits(slots_at(z + 2 * side), z - side)], axis=1)
    near_hits = jnp.concatenate([hits(slots_at(z + side), z), hits(slots_at(z + side), z - side)], axis=1)
    last_hits = hits(slots_at(jnp.where(z == 2, 3, 0)), z)
    own_hits = jnp.concatenate([hits(own_slots, z), hits(own_slots, z - side)], axis=1) * own_scale[:, None]


    step1[0] = slot(twos[0])
    pin(mid1[2])
    add_one(0)
    back_part = do(backward(late_use(own_ids), grad_out, adapter_up))
    with jax.named_scope("back_proj"):
        back_full = jnp.where((jnp.arange(dp_count) == z)[:, None, None], back_part.now, 0.0)
        back_full = lax.psum(back_full, ("dp", "tensor"))

    step1[1] = slot(twos[1])

    def terms():
        return [held.now[None] for held in (*up_terms, *moved_terms)]

    with jax.named_scope("far_terms"):
        far_sums = do(combine(late_use(far_hits), terms(), jnp.bfloat16))
        far_terms = Held(middle_hop(far_sums.now))
    pin(mid1[3])

    step2[0] = slot(ones[0], first_and_last_hop)
    add_late(0)
    add_one(1)

    step1[2] = slot(twos[2])
    add_late(1)
    pin(far_terms)
    with jax.named_scope("last_terms"):
        unit = jnp.ones((OWN_MAX,), jnp.float32)
        last_sums = do(combine(late_use(last_hits), terms()[:local_blocks], jnp.bfloat16, unit, [far_terms.now]))
        last_terms = Held(last_hop(last_sums.now))

    step1[3] = slot(twos[3])
    with jax.named_scope("near_terms"):
        near_sums = do(combine(late_use(near_hits), terms(), jnp.bfloat16))
        near_terms = Held(middle_hop(near_sums.now))
    pin(mid2[0])
    add_one(2)

    step2[1] = slot(ones[1], first_and_last_hop)
    pin(mid2[1])
    add_late(2)
    add_one(3)

    step2[2] = slot(ones[2], first_and_last_hop)
    pin(last_terms)
    add_late(3)
    backs = (SCALE * late_use(back_full)).astype(jnp.bfloat16)
    backs = [lax.dynamic_index_in_dim(backs, order[n], 0, keepdims=False) for n in range(dp_count)]
    grad_down = do(
        down_gradient(
            index, ids, inverse, [rows_first, rows_two, rows_one, rows_late], backs, adapter_down.shape
        )
    )

    step2[3] = slot(ones[3], first_and_last_hop)
    slot_gate[:] = chain[-2:-1]
    grad_up = do(combine(late_use(own_hits), terms(), jnp.float32, own_scale, [near_terms.now, last_terms.now]))
    own_mask = jnp.broadcast_to(
        (late_use(own_ids)[:, None] == tenant_ids[None, :])[:, None, :, None],
        (local_blocks, ROWS_BLK, tenants, rank_width),
    )
    wide = jnp.where(
        own_mask, projected.reshape(local_blocks, ROWS_BLK, 1, rank_width), jnp.zeros((), jnp.bfloat16)
    ).reshape(batch_rows, tenants * rank_width)
    layer_out = jnp.zeros((batch_rows, hidden), jnp.bfloat16)
    for j, (start, tiles) in enumerate(pieces):
        total = SCALE * jnp.dot(
            wide, flat_up[:, start * tile : (start + tiles) * tile], preferred_element_type=jnp.float32
        )
        total = total + jnp.where(outer, lates[j].now, firsts[j].now).astype(jnp.float32)
        total = total + mid2[j].now.astype(jnp.float32)
        total = total + step2[j].now.astype(jnp.float32)
        layer_out = lax.dynamic_update_slice(layer_out, total.astype(jnp.bfloat16), (0, start * tile))
    return (layer_out, grad_down.now, grad_up.now)


def local_plain(tokens, up_weight, adapter_down, adapter_up, grad_out, block_tenant, owner_of):
    dp_count = lax.axis_size("dp")
    dp_index = lax.axis_index("dp")
    tp_index = lax.axis_index("tensor")
    seq_rows, feature_count = tokens.shape
    batch_rows = grad_out.shape[0]
    local_blocks = batch_rows // ROWS_BLK
    all_blocks = local_blocks * dp_count
    column_part = feature_count // dp_count
    slice_cols = adapter_down.shape[2]
    rank_width = adapter_down.shape[1]
    tenants = adapter_down.shape[0]
    gathered = lax.all_gather(tokens, "tensor", axis=0, tiled=True)
    spread = lax.all_to_all(
        gathered.reshape(1, batch_rows, dp_count, column_part),
        "dp",
        split_axis=2,
        concat_axis=0,
        tiled=True,
    )
    all_rows = spread.reshape(dp_count * batch_rows, column_part)
    base_out = lax.psum_scatter(
        jnp.dot(all_rows, up_weight, preferred_element_type=jnp.float32).astype(jnp.bfloat16),
        "dp",
        scatter_dimension=0,
        tiled=True,
    ).astype(jnp.float32)
    slice_start = tp_index * slice_cols
    feature_slice = lax.dynamic_slice_in_dim(all_rows, slice_start, slice_cols, 1).reshape(
        all_blocks, ROWS_BLK, slice_cols
    )
    down_blocks = jnp.take(adapter_down, block_tenant, axis=0)
    proj_part = jnp.einsum(
        "nrd,nkd->nrk", feature_slice, down_blocks, preferred_element_type=jnp.float32
    )
    local_ids = lax.dynamic_slice_in_dim(block_tenant, dp_index * local_blocks, local_blocks, 0)
    up_mine = jnp.take(adapter_up, local_ids, axis=0)
    out_blocks = grad_out.reshape(local_blocks, ROWS_BLK, grad_out.shape[1])
    back_part = jnp.einsum("nrf,nkf->nrk", out_blocks, up_mine, preferred_element_type=jnp.float32)
    back_full = lax.dynamic_update_slice_in_dim(
        jnp.zeros((all_blocks, ROWS_BLK, rank_width), jnp.float32),
        back_part,
        dp_index * local_blocks,
        0,
    )
    proj_sum, back_sum = lax.psum(
        (proj_part.reshape(-1, 2 * rank_width), back_full.reshape(-1, 2 * rank_width)),
        ("dp", "tensor"),
    )
    projected = proj_sum.reshape(all_blocks, ROWS_BLK, rank_width).astype(jnp.bfloat16)
    back_proj = (SCALE * back_sum).reshape(all_blocks, ROWS_BLK, rank_width).astype(jnp.bfloat16)
    proj_mine = lax.dynamic_slice_in_dim(projected, dp_index * local_blocks, local_blocks, 0)
    adapter_term = jnp.einsum(
        "nrk,nkf->nrf", proj_mine, up_mine, preferred_element_type=jnp.float32
    ).reshape(batch_rows, -1)
    layer_out = (base_out + SCALE * adapter_term).astype(jnp.bfloat16)
    down_terms = jnp.einsum(
        "nrk,nrd->nkd", back_proj, feature_slice, preferred_element_type=jnp.float32
    )
    tenant_ids = jnp.arange(tenants, dtype=jnp.int32)
    onehot = (block_tenant[None, :] == tenant_ids[:, None]).astype(jnp.float32)
    inverse = 1.0 / jnp.sum(onehot, axis=1)
    grad_down = (
        jnp.einsum("tn,nkd->tkd", onehot, down_terms, precision=lax.Precision.HIGHEST)
        * inverse[:, None, None]
    )
    up_terms = SCALE * jnp.einsum(
        "nrk,nrf->nkf", proj_mine, out_blocks, preferred_element_type=jnp.float32
    )
    same_owner = owner_of[:, None] == owner_of[None, :]
    earlier = tenant_ids[None, :] < tenant_ids[:, None]
    rank_in = jnp.sum(jnp.logical_and(same_owner, earlier), axis=1)
    slot_of = owner_of * OWN_MAX + rank_in
    own_slots = dp_index * OWN_MAX + jnp.arange(OWN_MAX, dtype=jnp.int32)
    ownership = (slot_of[None, :] == own_slots[:, None]).astype(jnp.float32)
    own_scale = jnp.dot(ownership, inverse, precision=lax.Precision.HIGHEST)
    total_slots = dp_count * OWN_MAX
    local_slots = jnp.take(slot_of, local_ids, axis=0)
    placement = (local_slots[None, :] == jnp.arange(total_slots, dtype=jnp.int32)[:, None]).astype(
        jnp.float32
    )
    buffer = jnp.einsum("sn,nkf->skf", placement, up_terms, precision=lax.Precision.HIGHEST)
    summed = lax.psum_scatter(
        buffer.astype(jnp.bfloat16), "dp", scatter_dimension=0, tiled=True
    ).astype(jnp.float32)
    grad_up = summed * own_scale[:, None, None]
    return (layer_out, grad_down, grad_up)


def solution(mesh):
    placed = (
        P(("groups", "dp", "tensor"), None),
        P("dp", "tensor"),
        P("groups", None, ("dp", "tensor")),
        P("groups", None, "tensor"),
        P(("groups", "dp"), "tensor"),
        P("groups"),
        P("groups"),
    )
    return jax.shard_map(
        local if mesh.shape["dp"] == 4 else local_plain,
        mesh=mesh,
        in_specs=placed,
        out_specs=(
            P(("groups", "dp"), "tensor"),
            P("groups", None, ("dp", "tensor")),
            P(("groups", "dp"), None, "tensor"),
        ),
        check_vma=False,
    )
```

```python
import functools

import jax
import jax.numpy as jnp
from jax import lax
from jax.experimental import pallas as pl
from jax.experimental.pallas import tpu as pltpu
from jax.sharding import PartitionSpec as P

ROWS_BLK = 128
OWN_MAX = 2
SCALE = 0.5
SPLIT = ((0, 2), (2, 5), (5, 9), (9, 13))
WINDOW = 2
FULL = 5
VMEM = 60 * 1024 * 1024
ANY = pl.BlockSpec(memory_space=pl.ANY)
SMEM = pl.BlockSpec(memory_space=pltpu.SMEM)


class Held:
    def __init__(self, now):
        self.now = now


def tie(*held):
    distinct = list({id(one): one for one in held}.values())
    for one, now in zip(distinct, lax.optimization_barrier(tuple(one.now for one in distinct))):
        one.now = now


def after(value, *earlier):
    return lax.optimization_barrier((value, *earlier))[0]


def across(value, axis, bit):
    count = lax.axis_size(axis)
    return lax.ppermute(value, axis, [(i, i ^ bit) for i in range(count)])


def outward(value, hop):
    last = lax.axis_size("dp") - 1
    return lax.ppermute(value, "dp", [(hop, hop + 1), (last - hop, last - hop - 1)])


def bits_of(count):
    return [1 << k for k in reversed(range(count.bit_length() - 1))]


def gather_rows(rows):
    held = [(0, rows)]
    for bit in bits_of(lax.axis_size("tensor")):
        held = held + [(mask | bit, across(value, "tensor", bit)) for mask, value in held]
    return held


def sum_over_tensor(value):
    for bit in bits_of(lax.axis_size("tensor")):
        value = value + across(value, "tensor", bit)
    return value


def tile_of(width):
    return 512 if width % 512 == 0 else 128


def cut(width):
    tiles = width // tile_of(width)
    counts = [tiles * (i + 1) // 13 - tiles * i // 13 for i in range(13)]
    counts = [sum(counts[a:b]) for a, b in SPLIT]
    edges = [0]
    for n in counts:
        edges.append(edges[-1] + n)
    return list(zip(edges[:-1], counts))


def call(kernel, flops, **kwargs):
    return pl.pallas_call(
        kernel,
        compiler_params=pltpu.CompilerParams(vmem_limit_bytes=VMEM),
        cost_estimate=pl.CostEstimate(flops=10 * flops, bytes_accessed=0, transcendentals=0),
        **kwargs,
    )


def share_kernel(masks, has_add, deps, index, *refs):
    blocks, refs = refs[: len(masks)], refs[len(masks) :]
    weight, refs = refs[0], refs[1:]
    if has_add:
        arrived, refs = refs[0], refs[1:]
    out = refs[deps]
    batch = blocks[0]
    if len(masks) > 1:
        batch = refs[deps + 1]
        rows = blocks[0].shape[0]

        @pl.when(pl.program_id(0) == 0)
        def _():
            for mask, block in zip(masks, blocks):
                first = pl.multiple_of((index[0] ^ mask) * rows, rows)
                batch[pl.ds(first, rows), :] = block[...]

    value = jnp.dot(batch[...], weight[...], preferred_element_type=jnp.float32)
    if has_add:
        value = value + arrived[...].astype(jnp.float32)
    out[...] = value.astype(jnp.bfloat16)


def share(index, gathered, weight, piece, arrived=None, deps=()):
    masks, blocks = zip(*gathered)
    rows, depth = blocks[0].shape
    batch_rows = rows * len(blocks)
    tile = tile_of(weight.shape[1])
    first, count = piece
    column = pl.BlockSpec((batch_rows, tile), lambda i, s: (0, i))
    has_add = arrived is not None
    return call(
        functools.partial(share_kernel, masks, has_add, len(deps)),
        2 * batch_rows * depth * count * tile,
        out_shape=jax.ShapeDtypeStruct((batch_rows, count * tile), jnp.bfloat16),
        grid_spec=pltpu.PrefetchScalarGridSpec(
            num_scalar_prefetch=1,
            grid=(count,),
            in_specs=[pl.BlockSpec((rows, depth), lambda i, s: (0, 0))] * len(blocks)
            + [pl.BlockSpec((depth, tile), lambda i, s: (0, first + i))]
            + [column] * has_add
            + [ANY] * len(deps),
            out_specs=column,
            scratch_shapes=[pltpu.VMEM((batch_rows, depth), jnp.bfloat16)] * (len(blocks) > 1),
        ),
    )(index, *blocks, weight, *([arrived] if has_add else []), *deps)


def pair_kernel(deps, batch, weight, *refs):
    outs = refs[deps:]
    value = jnp.dot(batch[...], weight[...], preferred_element_type=jnp.float32)
    rows = outs[0].shape[0]
    for n, out in enumerate(outs):
        out[...] = value[n * rows : (n + 1) * rows].astype(jnp.bfloat16)


def pair(batches, weight, piece, deps):
    count_batches, rows, depth = batches.shape
    batch = batches.reshape(count_batches * rows, depth)
    tile = tile_of(weight.shape[1])
    first, count = piece
    column = pl.BlockSpec((rows, tile), lambda i: (0, i))
    return call(
        functools.partial(pair_kernel, len(deps)),
        2 * batch.size * count * tile,
        out_shape=[jax.ShapeDtypeStruct((rows, count * tile), jnp.bfloat16)] * count_batches,
        grid=(count,),
        in_specs=[
            pl.BlockSpec(batch.shape, lambda i: (0, 0)),
            pl.BlockSpec((depth, tile), lambda i: (0, first + i)),
        ]
        + [ANY] * len(deps),
        out_specs=[column] * count_batches,
    )(batch, weight, *deps)


def forward_kernel(count, deps, ids, *refs):
    blocks, down, outs = refs[:count], refs[count], refs[count + 1 + deps :]
    slices, _, _, width = down.shape
    for d in range(count):
        outs[d][...] = sum(
            lax.dot_general(
                blocks[d][:, n * width : (n + 1) * width],
                down[n, ids[d]],
                (((1,), (1,)), ((), ())),
                preferred_element_type=jnp.float32,
            )
            for n in range(slices)
        )


def forward(ids, blocks, down, deps):
    rows = blocks[0].shape[0]
    rank_width = down.shape[2]
    whole = pl.BlockSpec(memory_space=pltpu.VMEM)
    return call(
        functools.partial(forward_kernel, len(blocks), len(deps)),
        2 * len(blocks) * blocks[0].size * rank_width * 4,
        out_shape=[jax.ShapeDtypeStruct((rows, rank_width), jnp.float32)] * len(blocks),
        in_specs=[SMEM] + [whole] * (len(blocks) + 1) + [ANY] * len(deps),
        out_specs=[whole] * len(blocks),
    )(ids, *blocks, down, *deps)


def backward_kernel(ids, grad, up, out):
    @pl.when(pl.program_id(0) == 0)
    def _():
        out[...] = jnp.zeros_like(out)

    for b in range(grad.shape[0] // ROWS_BLK):
        rows = slice(b * ROWS_BLK, (b + 1) * ROWS_BLK)
        out[rows, :] += lax.dot_general(
            grad[rows, :], up[ids[b]], (((1,), (1,)), ((), ())), preferred_element_type=jnp.float32
        )


def backward(ids, grad_out, adapter_up):
    batch_rows, hidden = grad_out.shape
    tenants, rank_width, _ = adapter_up.shape
    tile = hidden // 4
    return call(
        backward_kernel,
        2 * batch_rows * hidden * rank_width * 4,
        out_shape=jax.ShapeDtypeStruct((batch_rows, rank_width), jnp.float32),
        grid_spec=pltpu.PrefetchScalarGridSpec(
            num_scalar_prefetch=1,
            grid=(hidden // tile,),
            in_specs=[
                pl.BlockSpec((batch_rows, tile), lambda i, n: (0, i)),
                pl.BlockSpec((tenants, rank_width, tile), lambda i, n: (0, 0, i)),
            ],
            out_specs=pl.BlockSpec((batch_rows, rank_width), lambda i, n: (0, 0)),
        ),
    )(ids, grad_out, adapter_up)


def down_kernel(masks, index, ids, inverse, *refs):
    out = refs[-1]
    out[...] = jnp.zeros_like(out)
    at = 0
    backs, refs = refs[: len(masks)], refs[len(masks) :]
    local_blocks = backs[0].shape[0] // ROWS_BLK
    for d, parts in enumerate(masks):
        for mask in parts:
            rows = refs[at].shape[0]
            first = 0 if len(parts) == 1 else pl.multiple_of((index[0] ^ mask) * rows, rows)
            step = min(rows, ROWS_BLK)
            for k in range(0, rows, step):
                tenant = ids[d * local_blocks + (first + k) // ROWS_BLK]
                out[tenant] += lax.dot_general(
                    backs[d][pl.ds(first + k, step), :],
                    refs[at][k : k + step, :],
                    (((0,), (0,)), ((), ())),
                    preferred_element_type=jnp.float32,
                )
            at += 1
    for n in range(out.shape[0]):
        out[n] *= inverse[n]


def down_gradient(index, ids, inverse, gathered, backs, shape):
    masks = [[mask for mask, _ in parts] for parts in gathered]
    arrays = [value for parts in gathered for _, value in parts]
    slice_cols = shape[2]
    return call(
        functools.partial(down_kernel, masks),
        8 * shape[1] * slice_cols * sum(value.shape[0] for value in arrays),
        out_shape=jax.ShapeDtypeStruct(shape, jnp.float32),
        grid_spec=pltpu.PrefetchScalarGridSpec(
            num_scalar_prefetch=2,
            grid=(1,),
            in_specs=[SMEM]
            + [pl.BlockSpec(back.shape, lambda i, s, n: (0, 0)) for back in backs]
            + [pl.BlockSpec((value.shape[0], slice_cols), lambda i, s, n: (0, s[0])) for value in arrays],
            out_specs=pl.BlockSpec(shape, lambda i, s, n: (0, 0, 0)),
        ),
    )(index, ids, inverse, *backs, *arrays)


def combine_kernel(count, extras, weights, scale, *refs):
    terms, more, out = refs[:count], refs[count : count + extras], refs[count + extras]
    parts = [term[0].astype(jnp.float32) for term in terms]
    for s in range(out.shape[0]):
        total = sum(part * weights[s, n] for n, part in enumerate(parts))
        if extras:
            total += sum(extra[s].astype(jnp.float32) for extra in more) * scale[s]
        out[s] = total.astype(out.dtype)


def combine(weights, terms, dtype, scale=None, extras=()):
    rank_width, hidden = terms[0].shape[1:]
    tile = hidden // 4
    slots = weights.shape[0]
    if scale is None:
        scale = jnp.ones((slots,), jnp.float32)
    return call(
        functools.partial(combine_kernel, len(terms), len(extras)),
        4 * slots * rank_width * hidden * len(terms),
        out_shape=jax.ShapeDtypeStruct((slots, rank_width, hidden), dtype),
        grid=(hidden // tile,),
        in_specs=[SMEM, SMEM]
        + [pl.BlockSpec((1, rank_width, tile), lambda i: (0, 0, i))] * len(terms)
        + [pl.BlockSpec((slots, rank_width, tile), lambda i: (0, 0, i))] * len(extras),
        out_specs=pl.BlockSpec((slots, rank_width, tile), lambda i: (0, 0, i)),
    )(weights, scale, *terms, *extras)


def local(tokens, up_weight, adapter_down, adapter_up, grad_out, block_tenant, owner_of):
    dp_count = 4
    z = lax.axis_index("dp")
    t = lax.axis_index("tensor")
    outer = jnp.logical_or(z == 0, z == 3)
    part_rows, feature_count = tokens.shape
    batch_rows, hidden = grad_out.shape
    local_blocks = batch_rows // ROWS_BLK
    depth = feature_count // dp_count
    tenants, rank_width, slice_cols = adapter_down.shape
    flat_up = adapter_up.reshape(tenants * rank_width, hidden)
    pieces = cut(hidden)
    tile = tile_of(hidden)
    index = t.reshape(1)

    def block_for(where):
        return lax.dynamic_slice_in_dim(tokens, where * depth, depth, 1)

    def first_hop(value):
        return lax.ppermute(value, "dp", [(0, 1), (3, 2)])

    def middle_hop(value):
        return lax.ppermute(value, "dp", [(1, 2), (2, 1)])

    def last_hop(value):
        return lax.ppermute(value, "dp", [(1, 0), (2, 3)])

    def first_and_last_hop(value):
        return lax.ppermute(value, "dp", [(0, 1), (3, 2), (1, 0), (2, 3)])

    def gather(value):
        return [(0, lax.all_gather(value, "tensor", axis=0, tiled=True))]

    down_all = lax.all_gather(adapter_down, "tensor", axis=0)
    far = lax.ppermute(block_for(z ^ 3), "dp", [(0, 3), (3, 0)])
    two = across(block_for(z ^ 2), "dp", 2)
    one = across(block_for(z ^ 1), "dp", 1)
    far, one = lax.optimization_barrier((far, one))
    middle = middle_hop(after(block_for(z ^ 3), far))
    mine = block_for(z)
    first_part = jnp.where(outer, far, mine)
    with jax.named_scope("first_rows"):
        other_chip = across(first_part, "tensor", 2)
        other_chip, two = lax.optimization_barrier((other_chip, two))
        rows_first = [
            (0, first_part),
            (2, other_chip),
            (1, across(first_part, "tensor", 1)),
            (3, across(other_chip, "tensor", 1)),
        ]

    chain = []
    work, earlier_work, pinned = [], [], []
    slot_gate = []

    def slot(value, hop=first_hop):
        k = len(chain)
        at = max(k - WINDOW, 0)
        slot_gate[:] = chain[at : at + 1]
        with jax.named_scope(f"send{k}"):
            tie(value, *slot_gate, *pinned, *(work[-1:] if k >= FULL else earlier_work))
            chain.append(Held(hop(value.now)))
        earlier_work[:] = work[-1:]
        pinned.clear()
        return chain[-1]

    def pin(arrived):
        pinned.append(arrived)

    def do(value):
        work.append(Held(value))
        return work[-1]

    def late_use(value):
        held = Held(value)
        tie(held, *slot_gate, *work[-1:])
        return held.now

    def piece_of(name, rows, j, arrived=None):
        arrived = arrived if arrived is None else arrived.now
        deps = [held.now for held in (*slot_gate, *work[-1:])]
        with jax.named_scope(f"{name}{j}"):
            return do(share(index, rows, up_weight, pieces[j], arrived=arrived, deps=deps))

    firsts, twos, ones, lates = {}, {}, {}, {}
    step0, step1, step2, mid1, mid2 = {}, {}, {}, {}, {}

    def two_of(j):
        twos[j] = piece_of("two", rows_two, j, step0[j])
        with jax.named_scope(f"mid_two{j}"):
            mid1[j] = Held(middle_hop(twos[j].now))

    def pair_of(j):
        with jax.named_scope(f"pair{j}"):
            deps = [held.now for held in (*slot_gate, *work[-1:])]
            ones[j], lates[j] = map(Held, pair(rows_pair, up_weight, pieces[j], deps))
            work.append(lates[j])

    def add(own, arrived):
        tie(own, arrived, *slot_gate, *work[-1:])
        return do((own.now.astype(jnp.float32) + arrived.now.astype(jnp.float32)).astype(jnp.bfloat16))

    def add_late(j):
        with jax.named_scope(f"late{j}"):
            mid2[j] = Held(middle_hop(add(lates[j], step1[j]).now))

    def add_one(j):
        with jax.named_scope(f"one{j}"):
            ones[j] = add(ones[j], mid1[j])

    with jax.named_scope("two_rows"):
        rows_two = gather(two)
    firsts[0] = piece_of("first", rows_first, 0)

    step0[0] = slot(firsts[0])
    firsts[1] = piece_of("first", rows_first, 1)
    with jax.named_scope("rest_rows"):
        late_part = jnp.where(outer, mine, late_use(middle))
        rows_pair = lax.all_gather(jnp.stack([one, late_part]), "tensor", axis=1, tiled=True)
    block_tenant = late_use(block_tenant)

    step0[1] = slot(firsts[1])
    slot_gate[:] = chain[:1]

    tenant_ids = jnp.arange(tenants, dtype=jnp.int32)
    order = jnp.stack([jnp.where(outer, z ^ 3, z), z ^ 2, z ^ 1, jnp.where(outer, z, z ^ 3)])
    blocks_of = block_tenant.reshape(dp_count, local_blocks)
    ids = jnp.take(blocks_of, order, axis=0)
    row_ids = lax.dynamic_index_in_dim(ids, t * part_rows // ROWS_BLK, 1, keepdims=False)
    ids = ids.reshape(-1)
    own_ids = lax.dynamic_index_in_dim(blocks_of, z, 0, keepdims=False)
    with jax.named_scope("forward"):
        parts = jnp.stack(forward(late_use(row_ids), [first_part, two, one, late_part], down_all, ()))
        by_batch = jnp.where((order[None, :] == jnp.arange(dp_count)[:, None])[:, :, None, None], parts, 0.0)
        by_batch = do(jnp.sum(by_batch, axis=1)).now
        projected = lax.psum_scatter(by_batch, "dp", scatter_dimension=0, tiled=True)[0]
    firsts[2] = piece_of("first", rows_first, 2)

    step0[2] = slot(firsts[2])
    slot_gate[:] = chain[1:2]
    firsts[3] = piece_of("first", rows_first, 3)
    two_of(0)

    step0[3] = slot(firsts[3])
    with jax.named_scope("projected"):
        projected = late_use(projected).astype(jnp.bfloat16)
        projected = lax.all_gather(projected, "tensor", axis=0, tiled=True)
    two_of(1)
    projected = late_use(projected)
    up_terms = []
    for b in range(local_blocks):
        rows = slice(b * ROWS_BLK, (b + 1) * ROWS_BLK)
        term = SCALE * lax.dot_general(
            projected[rows], grad_out[rows], (((0,), (0,)), ((), ())), preferred_element_type=jnp.float32
        )
        up_terms.append(do(term.astype(jnp.bfloat16)))

    moved_terms = [slot(up_terms[0])]
    two_of(2)
    pair_of(0)
    pair_of(1)
    pin(mid1[0])

    moved_terms.append(slot(up_terms[1]))
    two_of(3)
    pair_of(2)
    pin(mid1[1])
    owner_of = late_use(owner_of)
    onehot = (block_tenant[None, :] == tenant_ids[:, None]).astype(jnp.float32)
    inverse = 1.0 / jnp.sum(onehot, axis=1)
    same_owner = owner_of[:, None] == owner_of[None, :]
    earlier = tenant_ids[None, :] < tenant_ids[:, None]
    slot_of = owner_of * OWN_MAX + jnp.sum(jnp.logical_and(same_owner, earlier), axis=1)
    own_slots = z * OWN_MAX + jnp.arange(OWN_MAX, dtype=jnp.int32)
    ownership = (slot_of[None, :] == own_slots[:, None]).astype(jnp.float32)
    own_scale = jnp.sum(ownership * inverse[None, :], axis=1)
    block_slot = jnp.sum(
        jnp.where(block_tenant[:, None] == tenant_ids[None, :], slot_of[None, :], 0), axis=1
    ).reshape(dp_count, local_blocks)

    def hits(slots, batch):
        theirs = lax.dynamic_index_in_dim(block_slot, jnp.clip(batch, 0, 3), 0, keepdims=False)
        return (slots[:, None] == theirs[None, :]).astype(jnp.float32)

    def slots_at(where):
        return where * OWN_MAX + jnp.arange(OWN_MAX, dtype=jnp.int32)

    side = jnp.where(z == 1, 1, -1)
    far_hits = jnp.concatenate([hits(slots_at(z + 2 * side), z), hits(slots_at(z + 2 * side), z - side)], axis=1)
    near_hits = jnp.concatenate([hits(slots_at(z + side), z), hits(slots_at(z + side), z - side)], axis=1)
    last_hits = hits(slots_at(jnp.where(z == 2, 3, 0)), z)
    own_hits = jnp.concatenate([hits(own_slots, z), hits(own_slots, z - side)], axis=1) * own_scale[:, None]


    step1[0] = slot(twos[0])
    pin(mid1[2])
    pair_of(3)
    add_one(0)
    back_part = do(backward(late_use(own_ids), grad_out, adapter_up))
    with jax.named_scope("back_proj"):
        back_full = jnp.where((jnp.arange(dp_count) == z)[:, None, None], back_part.now, 0.0)
        back_full = lax.psum(back_full, ("dp", "tensor"))

    step1[1] = slot(twos[1])

    def terms():
        return [held.now[None] for held in (*up_terms, *moved_terms)]

    with jax.named_scope("far_terms"):
        far_sums = do(combine(late_use(far_hits), terms(), jnp.bfloat16))
        far_terms = Held(middle_hop(far_sums.now))
    pin(mid1[3])

    step2[0] = slot(ones[0], first_and_last_hop)
    add_late(0)
    add_one(1)

    step1[2] = slot(twos[2])
    add_late(1)
    pin(far_terms)
    with jax.named_scope("last_terms"):
        unit = jnp.ones((OWN_MAX,), jnp.float32)
        last_sums = do(combine(late_use(last_hits), terms()[:local_blocks], jnp.bfloat16, unit, [far_terms.now]))
        last_terms = Held(last_hop(last_sums.now))

    step1[3] = slot(twos[3])
    with jax.named_scope("near_terms"):
        near_sums = do(combine(late_use(near_hits), terms(), jnp.bfloat16))
        near_terms = Held(middle_hop(near_sums.now))
    pin(mid2[0])
    add_one(2)

    step2[1] = slot(ones[1], first_and_last_hop)
    pin(mid2[1])
    add_late(2)
    add_one(3)

    step2[2] = slot(ones[2], first_and_last_hop)
    pin(last_terms)
    add_late(3)
    backs = (SCALE * late_use(back_full)).astype(jnp.bfloat16)
    backs = [lax.dynamic_index_in_dim(backs, order[n], 0, keepdims=False) for n in range(dp_count)]
    grad_down = do(
        down_gradient(
            index, ids, inverse, [rows_first, rows_two, *([(0, rows)] for rows in rows_pair)], backs, adapter_down.shape
        )
    )

    step2[3] = slot(ones[3], first_and_last_hop)
    slot_gate[:] = chain[-2:-1]
    grad_up = do(combine(late_use(own_hits), terms(), jnp.float32, own_scale, [near_terms.now, last_terms.now]))
    own_mask = jnp.broadcast_to(
        (late_use(own_ids)[:, None] == tenant_ids[None, :])[:, None, :, None],
        (local_blocks, ROWS_BLK, tenants, rank_width),
    )
    wide = jnp.where(
        own_mask, projected.reshape(local_blocks, ROWS_BLK, 1, rank_width), jnp.zeros((), jnp.bfloat16)
    ).reshape(batch_rows, tenants * rank_width)
    layer_out = jnp.zeros((batch_rows, hidden), jnp.bfloat16)
    for j, (start, tiles) in enumerate(pieces):
        total = SCALE * jnp.dot(
            wide, flat_up[:, start * tile : (start + tiles) * tile], preferred_element_type=jnp.float32
        )
        total = total + jnp.where(outer, lates[j].now, firsts[j].now).astype(jnp.float32)
        total = total + mid2[j].now.astype(jnp.float32)
        total = total + step2[j].now.astype(jnp.float32)
        layer_out = lax.dynamic_update_slice(layer_out, total.astype(jnp.bfloat16), (0, start * tile))
    return (layer_out, grad_down.now, grad_up.now)


def local_plain(tokens, up_weight, adapter_down, adapter_up, grad_out, block_tenant, owner_of):
    dp_count = lax.axis_size("dp")
    dp_index = lax.axis_index("dp")
    tp_index = lax.axis_index("tensor")
    seq_rows, feature_count = tokens.shape
    batch_rows = grad_out.shape[0]
    local_blocks = batch_rows // ROWS_BLK
    all_blocks = local_blocks * dp_count
    column_part = feature_count // dp_count
    slice_cols = adapter_down.shape[2]
    rank_width = adapter_down.shape[1]
    tenants = adapter_down.shape[0]
    gathered = lax.all_gather(tokens, "tensor", axis=0, tiled=True)
    spread = lax.all_to_all(
        gathered.reshape(1, batch_rows, dp_count, column_part),
        "dp",
        split_axis=2,
        concat_axis=0,
        tiled=True,
    )
    all_rows = spread.reshape(dp_count * batch_rows, column_part)
    base_out = lax.psum_scatter(
        jnp.dot(all_rows, up_weight, preferred_element_type=jnp.float32).astype(jnp.bfloat16),
        "dp",
        scatter_dimension=0,
        tiled=True,
    ).astype(jnp.float32)
    slice_start = tp_index * slice_cols
    feature_slice = lax.dynamic_slice_in_dim(all_rows, slice_start, slice_cols, 1).reshape(
        all_blocks, ROWS_BLK, slice_cols
    )
    down_blocks = jnp.take(adapter_down, block_tenant, axis=0)
    proj_part = jnp.einsum(
        "nrd,nkd->nrk", feature_slice, down_blocks, preferred_element_type=jnp.float32
    )
    local_ids = lax.dynamic_slice_in_dim(block_tenant, dp_index * local_blocks, local_blocks, 0)
    up_mine = jnp.take(adapter_up, local_ids, axis=0)
    out_blocks = grad_out.reshape(local_blocks, ROWS_BLK, grad_out.shape[1])
    back_part = jnp.einsum("nrf,nkf->nrk", out_blocks, up_mine, preferred_element_type=jnp.float32)
    back_full = lax.dynamic_update_slice_in_dim(
        jnp.zeros((all_blocks, ROWS_BLK, rank_width), jnp.float32),
        back_part,
        dp_index * local_blocks,
        0,
    )
    proj_sum, back_sum = lax.psum(
        (proj_part.reshape(-1, 2 * rank_width), back_full.reshape(-1, 2 * rank_width)),
        ("dp", "tensor"),
    )
    projected = proj_sum.reshape(all_blocks, ROWS_BLK, rank_width).astype(jnp.bfloat16)
    back_proj = (SCALE * back_sum).reshape(all_blocks, ROWS_BLK, rank_width).astype(jnp.bfloat16)
    proj_mine = lax.dynamic_slice_in_dim(projected, dp_index * local_blocks, local_blocks, 0)
    adapter_term = jnp.einsum(
        "nrk,nkf->nrf", proj_mine, up_mine, preferred_element_type=jnp.float32
    ).reshape(batch_rows, -1)
    layer_out = (base_out + SCALE * adapter_term).astype(jnp.bfloat16)
    down_terms = jnp.einsum(
        "nrk,nrd->nkd", back_proj, feature_slice, preferred_element_type=jnp.float32
    )
    tenant_ids = jnp.arange(tenants, dtype=jnp.int32)
    onehot = (block_tenant[None, :] == tenant_ids[:, None]).astype(jnp.float32)
    inverse = 1.0 / jnp.sum(onehot, axis=1)
    grad_down = (
        jnp.einsum("tn,nkd->tkd", onehot, down_terms, precision=lax.Precision.HIGHEST)
        * inverse[:, None, None]
    )
    up_terms = SCALE * jnp.einsum(
        "nrk,nrf->nkf", proj_mine, out_blocks, preferred_element_type=jnp.float32
    )
    same_owner = owner_of[:, None] == owner_of[None, :]
    earlier = tenant_ids[None, :] < tenant_ids[:, None]
    rank_in = jnp.sum(jnp.logical_and(same_owner, earlier), axis=1)
    slot_of = owner_of * OWN_MAX + rank_in
    own_slots = dp_index * OWN_MAX + jnp.arange(OWN_MAX, dtype=jnp.int32)
    ownership = (slot_of[None, :] == own_slots[:, None]).astype(jnp.float32)
    own_scale = jnp.dot(ownership, inverse, precision=lax.Precision.HIGHEST)
    total_slots = dp_count * OWN_MAX
    local_slots = jnp.take(slot_of, local_ids, axis=0)
    placement = (local_slots[None, :] == jnp.arange(total_slots, dtype=jnp.int32)[:, None]).astype(
        jnp.float32
    )
    buffer = jnp.einsum("sn,nkf->skf", placement, up_terms, precision=lax.Precision.HIGHEST)
    summed = lax.psum_scatter(
        buffer.astype(jnp.bfloat16), "dp", scatter_dimension=0, tiled=True
    ).astype(jnp.float32)
    grad_up = summed * own_scale[:, None, None]
    return (layer_out, grad_down, grad_up)


def solution(mesh):
    placed = (
        P(("groups", "dp", "tensor"), None),
        P("dp", "tensor"),
        P("groups", None, ("dp", "tensor")),
        P("groups", None, "tensor"),
        P(("groups", "dp"), "tensor"),
        P("groups"),
        P("groups"),
    )
    return jax.shard_map(
        local if mesh.shape["dp"] == 4 else local_plain,
        mesh=mesh,
        in_specs=placed,
        out_specs=(
            P(("groups", "dp"), "tensor"),
            P("groups", None, ("dp", "tensor")),
            P(("groups", "dp"), None, "tensor"),
        ),
        check_vma=False,
    )
```

```python
import functools

import jax
import jax.numpy as jnp
from jax import lax
from jax.experimental import pallas as pl
from jax.experimental.pallas import tpu as pltpu
from jax.sharding import PartitionSpec as P

ROWS_BLK = 128
OWN_MAX = 2
SCALE = 0.5
SPLIT = ((0, 2), (2, 5), (5, 9), (9, 13))
WINDOW = 2
FULL = 5
VMEM = 60 * 1024 * 1024
ANY = pl.BlockSpec(memory_space=pl.ANY)
SMEM = pl.BlockSpec(memory_space=pltpu.SMEM)


class Held:
    def __init__(self, now):
        self.now = now


def tie(*held):
    distinct = list({id(one): one for one in held}.values())
    for one, now in zip(distinct, lax.optimization_barrier(tuple(one.now for one in distinct))):
        one.now = now


def after(value, *earlier):
    return lax.optimization_barrier((value, *earlier))[0]


def across(value, axis, bit):
    count = lax.axis_size(axis)
    return lax.ppermute(value, axis, [(i, i ^ bit) for i in range(count)])


def outward(value, hop):
    last = lax.axis_size("dp") - 1
    return lax.ppermute(value, "dp", [(hop, hop + 1), (last - hop, last - hop - 1)])


def bits_of(count):
    return [1 << k for k in reversed(range(count.bit_length() - 1))]


def gather_rows(rows):
    held = [(0, rows)]
    for bit in bits_of(lax.axis_size("tensor")):
        held = held + [(mask | bit, across(value, "tensor", bit)) for mask, value in held]
    return held


def sum_over_tensor(value):
    for bit in bits_of(lax.axis_size("tensor")):
        value = value + across(value, "tensor", bit)
    return value


def tile_of(width):
    return 512 if width % 512 == 0 else 128


def cut(width):
    tiles = width // tile_of(width)
    counts = [tiles * (i + 1) // 13 - tiles * i // 13 for i in range(13)]
    counts = [sum(counts[a:b]) for a, b in SPLIT]
    edges = [0]
    for n in counts:
        edges.append(edges[-1] + n)
    return list(zip(edges[:-1], counts))


def call(kernel, flops, **kwargs):
    return pl.pallas_call(
        kernel,
        compiler_params=pltpu.CompilerParams(vmem_limit_bytes=VMEM),
        cost_estimate=pl.CostEstimate(flops=10 * flops, bytes_accessed=0, transcendentals=0),
        **kwargs,
    )


def share_kernel(masks, has_add, deps, index, *refs):
    blocks, refs = refs[: len(masks)], refs[len(masks) :]
    weight, refs = refs[0], refs[1:]
    if has_add:
        arrived, refs = refs[0], refs[1:]
    out = refs[deps]
    batch = blocks[0]
    if len(masks) > 1:
        batch = refs[deps + 1]
        rows = blocks[0].shape[0]

        @pl.when(pl.program_id(0) == 0)
        def _():
            for mask, block in zip(masks, blocks):
                first = pl.multiple_of((index[0] ^ mask) * rows, rows)
                batch[pl.ds(first, rows), :] = block[...]

    value = jnp.dot(batch[...], weight[...], preferred_element_type=jnp.float32)
    if has_add:
        value = value + arrived[...].astype(jnp.float32)
    out[...] = value.astype(jnp.bfloat16)


def share(index, gathered, weight, piece, arrived=None, deps=()):
    masks, blocks = zip(*gathered)
    rows, depth = blocks[0].shape
    batch_rows = rows * len(blocks)
    tile = tile_of(weight.shape[1])
    first, count = piece
    column = pl.BlockSpec((batch_rows, tile), lambda i, s: (0, i))
    has_add = arrived is not None
    return call(
        functools.partial(share_kernel, masks, has_add, len(deps)),
        2 * batch_rows * depth * count * tile,
        out_shape=jax.ShapeDtypeStruct((batch_rows, count * tile), jnp.bfloat16),
        grid_spec=pltpu.PrefetchScalarGridSpec(
            num_scalar_prefetch=1,
            grid=(count,),
            in_specs=[pl.BlockSpec((rows, depth), lambda i, s: (0, 0))] * len(blocks)
            + [pl.BlockSpec((depth, tile), lambda i, s: (0, first + i))]
            + [column] * has_add
            + [ANY] * len(deps),
            out_specs=column,
            scratch_shapes=[pltpu.VMEM((batch_rows, depth), jnp.bfloat16)] * (len(blocks) > 1),
        ),
    )(index, *blocks, weight, *([arrived] if has_add else []), *deps)


def pair_kernel(deps, batch, weight, *refs):
    outs = refs[deps:]
    value = jnp.dot(batch[...], weight[...], preferred_element_type=jnp.float32)
    rows = outs[0].shape[0]
    for n, out in enumerate(outs):
        out[...] = value[n * rows : (n + 1) * rows].astype(jnp.bfloat16)


def pair(batches, weight, piece, deps):
    count_batches, rows, depth = batches.shape
    batch = batches.reshape(count_batches * rows, depth)
    tile = tile_of(weight.shape[1])
    first, count = piece
    column = pl.BlockSpec((rows, tile), lambda i: (0, i))
    return call(
        functools.partial(pair_kernel, len(deps)),
        2 * batch.size * count * tile,
        out_shape=[jax.ShapeDtypeStruct((rows, count * tile), jnp.bfloat16)] * count_batches,
        grid=(count,),
        in_specs=[
            pl.BlockSpec(batch.shape, lambda i: (0, 0)),
            pl.BlockSpec((depth, tile), lambda i: (0, first + i)),
        ]
        + [ANY] * len(deps),
        out_specs=[column] * count_batches,
    )(batch, weight, *deps)


def forward_kernel(count, deps, ids, *refs):
    blocks, down, outs = refs[:count], refs[count], refs[count + 1 + deps :]
    slices, _, _, width = down.shape
    for d in range(count):
        outs[d][...] = sum(
            lax.dot_general(
                blocks[d][:, n * width : (n + 1) * width],
                down[n, ids[d]],
                (((1,), (1,)), ((), ())),
                preferred_element_type=jnp.float32,
            )
            for n in range(slices)
        )


def forward(ids, blocks, down, deps):
    rows = blocks[0].shape[0]
    rank_width = down.shape[2]
    whole = pl.BlockSpec(memory_space=pltpu.VMEM)
    return call(
        functools.partial(forward_kernel, len(blocks), len(deps)),
        2 * len(blocks) * blocks[0].size * rank_width * 4,
        out_shape=[jax.ShapeDtypeStruct((rows, rank_width), jnp.float32)] * len(blocks),
        in_specs=[SMEM] + [whole] * (len(blocks) + 1) + [ANY] * len(deps),
        out_specs=[whole] * len(blocks),
    )(ids, *blocks, down, *deps)


def backward_kernel(ids, grad, up, out):
    @pl.when(pl.program_id(0) == 0)
    def _():
        out[...] = jnp.zeros_like(out)

    for b in range(grad.shape[0] // ROWS_BLK):
        rows = slice(b * ROWS_BLK, (b + 1) * ROWS_BLK)
        out[rows, :] += lax.dot_general(
            grad[rows, :], up[ids[b]], (((1,), (1,)), ((), ())), preferred_element_type=jnp.float32
        )


def backward(ids, grad_out, adapter_up):
    batch_rows, hidden = grad_out.shape
    tenants, rank_width, _ = adapter_up.shape
    tile = hidden // 4
    return call(
        backward_kernel,
        2 * batch_rows * hidden * rank_width * 4,
        out_shape=jax.ShapeDtypeStruct((batch_rows, rank_width), jnp.float32),
        grid_spec=pltpu.PrefetchScalarGridSpec(
            num_scalar_prefetch=1,
            grid=(hidden // tile,),
            in_specs=[
                pl.BlockSpec((batch_rows, tile), lambda i, n: (0, i)),
                pl.BlockSpec((tenants, rank_width, tile), lambda i, n: (0, 0, i)),
            ],
            out_specs=pl.BlockSpec((batch_rows, rank_width), lambda i, n: (0, 0)),
        ),
    )(ids, grad_out, adapter_up)


def down_kernel(masks, index, ids, inverse, *refs):
    out = refs[-1]
    out[...] = jnp.zeros_like(out)
    at = 0
    backs, refs = refs[: len(masks)], refs[len(masks) :]
    local_blocks = backs[0].shape[0] // ROWS_BLK
    for d, parts in enumerate(masks):
        for mask in parts:
            rows = refs[at].shape[0]
            first = 0 if len(parts) == 1 else pl.multiple_of((index[0] ^ mask) * rows, rows)
            step = min(rows, ROWS_BLK)
            for k in range(0, rows, step):
                tenant = ids[d * local_blocks + (first + k) // ROWS_BLK]
                out[tenant] += lax.dot_general(
                    backs[d][pl.ds(first + k, step), :],
                    refs[at][k : k + step, :],
                    (((0,), (0,)), ((), ())),
                    preferred_element_type=jnp.float32,
                )
            at += 1
    for n in range(out.shape[0]):
        out[n] *= inverse[n]


def down_gradient(index, ids, inverse, gathered, backs, shape):
    masks = [[mask for mask, _ in parts] for parts in gathered]
    arrays = [value for parts in gathered for _, value in parts]
    slice_cols = shape[2]
    return call(
        functools.partial(down_kernel, masks),
        8 * shape[1] * slice_cols * sum(value.shape[0] for value in arrays),
        out_shape=jax.ShapeDtypeStruct(shape, jnp.float32),
        grid_spec=pltpu.PrefetchScalarGridSpec(
            num_scalar_prefetch=2,
            grid=(1,),
            in_specs=[SMEM]
            + [pl.BlockSpec(back.shape, lambda i, s, n: (0, 0)) for back in backs]
            + [pl.BlockSpec((value.shape[0], slice_cols), lambda i, s, n: (0, s[0])) for value in arrays],
            out_specs=pl.BlockSpec(shape, lambda i, s, n: (0, 0, 0)),
        ),
    )(index, ids, inverse, *backs, *arrays)


def combine_kernel(count, extras, weights, scale, *refs):
    terms, more, out = refs[:count], refs[count : count + extras], refs[count + extras]
    parts = [term[0].astype(jnp.float32) for term in terms]
    for s in range(out.shape[0]):
        total = sum(part * weights[s, n] for n, part in enumerate(parts))
        if extras:
            total += sum(extra[s].astype(jnp.float32) for extra in more) * scale[s]
        out[s] = total.astype(out.dtype)


def combine(weights, terms, dtype, scale=None, extras=()):
    rank_width, hidden = terms[0].shape[1:]
    tile = hidden // 4
    slots = weights.shape[0]
    if scale is None:
        scale = jnp.ones((slots,), jnp.float32)
    return call(
        functools.partial(combine_kernel, len(terms), len(extras)),
        4 * slots * rank_width * hidden * len(terms),
        out_shape=jax.ShapeDtypeStruct((slots, rank_width, hidden), dtype),
        grid=(hidden // tile,),
        in_specs=[SMEM, SMEM]
        + [pl.BlockSpec((1, rank_width, tile), lambda i: (0, 0, i))] * len(terms)
        + [pl.BlockSpec((slots, rank_width, tile), lambda i: (0, 0, i))] * len(extras),
        out_specs=pl.BlockSpec((slots, rank_width, tile), lambda i: (0, 0, i)),
    )(weights, scale, *terms, *extras)


def local(tokens, up_weight, adapter_down, adapter_up, grad_out, block_tenant, owner_of):
    dp_count = 4
    z = lax.axis_index("dp")
    t = lax.axis_index("tensor")
    outer = jnp.logical_or(z == 0, z == 3)
    part_rows, feature_count = tokens.shape
    batch_rows, hidden = grad_out.shape
    local_blocks = batch_rows // ROWS_BLK
    depth = feature_count // dp_count
    tenants, rank_width, slice_cols = adapter_down.shape
    flat_up = adapter_up.reshape(tenants * rank_width, hidden)
    pieces = cut(hidden)
    tile = tile_of(hidden)
    index = t.reshape(1)

    def block_for(where):
        return lax.dynamic_slice_in_dim(tokens, where * depth, depth, 1)

    def first_hop(value):
        return lax.ppermute(value, "dp", [(0, 1), (3, 2)])

    def middle_hop(value):
        return lax.ppermute(value, "dp", [(1, 2), (2, 1)])

    def last_hop(value):
        return lax.ppermute(value, "dp", [(1, 0), (2, 3)])

    def first_and_last_hop(value):
        return lax.ppermute(value, "dp", [(0, 1), (3, 2), (1, 0), (2, 3)])

    def gather(value):
        return [(0, lax.all_gather(value, "tensor", axis=0, tiled=True))]

    down_all = lax.all_gather(adapter_down, "tensor", axis=0)
    far = lax.ppermute(block_for(z ^ 3), "dp", [(0, 3), (3, 0)])
    two = across(block_for(z ^ 2), "dp", 2)
    one = across(block_for(z ^ 1), "dp", 1)
    far, one = lax.optimization_barrier((far, one))
    middle = middle_hop(after(block_for(z ^ 3), far))
    mine = block_for(z)
    first_part = jnp.where(outer, far, mine)
    with jax.named_scope("first_rows"):
        other_chip = across(first_part, "tensor", 2)
        other_chip, two = lax.optimization_barrier((other_chip, two))
        rows_first = [
            (0, first_part),
            (2, other_chip),
            (1, across(first_part, "tensor", 1)),
            (3, across(other_chip, "tensor", 1)),
        ]

    chain = []
    work, earlier_work, pinned = [], [], []
    slot_gate = []

    def slot(value, hop=first_hop):
        k = len(chain)
        at = max(k - WINDOW, 0)
        slot_gate[:] = chain[at : at + 1]
        with jax.named_scope(f"send{k}"):
            tie(value, *slot_gate, *pinned, *earlier_work)
            chain.append(Held(hop(value.now)))
        earlier_work[:] = work[-1:]
        pinned.clear()
        return chain[-1]

    def pin(arrived):
        pinned.append(arrived)

    def do(value):
        work.append(Held(value))
        return work[-1]

    def late_use(value):
        held = Held(value)
        tie(held, *slot_gate, *work[-1:])
        return held.now

    def piece_of(name, rows, j, arrived=None):
        arrived = arrived if arrived is None else arrived.now
        deps = [held.now for held in (*slot_gate, *work[-1:])]
        with jax.named_scope(f"{name}{j}"):
            return do(share(index, rows, up_weight, pieces[j], arrived=arrived, deps=deps))

    firsts, twos, ones, lates = {}, {}, {}, {}
    step0, step1, step2, mid1, mid2 = {}, {}, {}, {}, {}

    def add_two(j):
        twos[j] = piece_of("two", rows_two, j, step0[j])
        with jax.named_scope(f"mid_two{j}"):
            mid1[j] = Held(middle_hop(twos[j].now))

    def add_late(j):
        lates[j] = piece_of("late", rows_late, j, step1[j])
        with jax.named_scope(f"mid_late{j}"):
            mid2[j] = Held(middle_hop(lates[j].now))

    def add_one(j):
        ones[j] = piece_of("one", rows_one, j, mid1[j])

    with jax.named_scope("two_rows"):
        rows_two = gather(two)
    firsts[0] = piece_of("first", rows_first, 0)
    step0[0] = slot(firsts[0])
    firsts[1] = piece_of("first", rows_first, 1)
    with jax.named_scope("one_rows"):
        one = late_use(one)
        rows_one = gather(one)
    with jax.named_scope("late_rows"):
        late_part = jnp.where(outer, mine, late_use(middle))
        rows_late = gather(late_part)
    block_tenant = late_use(block_tenant)

    step0[1] = slot(firsts[1])
    slot_gate[:] = chain[:1]

    tenant_ids = jnp.arange(tenants, dtype=jnp.int32)
    order = jnp.stack([jnp.where(outer, z ^ 3, z), z ^ 2, z ^ 1, jnp.where(outer, z, z ^ 3)])
    blocks_of = block_tenant.reshape(dp_count, local_blocks)
    ids = jnp.take(blocks_of, order, axis=0)
    row_ids = lax.dynamic_index_in_dim(ids, t * part_rows // ROWS_BLK, 1, keepdims=False)
    ids = ids.reshape(-1)
    own_ids = lax.dynamic_index_in_dim(blocks_of, z, 0, keepdims=False)
    with jax.named_scope("forward"):
        parts = jnp.stack(forward(late_use(row_ids), [first_part, two, one, late_part], down_all, ()))
        by_batch = jnp.where((order[None, :] == jnp.arange(dp_count)[:, None])[:, :, None, None], parts, 0.0)
        by_batch = do(jnp.sum(by_batch, axis=1)).now
        projected = lax.psum_scatter(by_batch, "dp", scatter_dimension=0, tiled=True)[0]
    firsts[2] = piece_of("first", rows_first, 2)

    step0[2] = slot(firsts[2])
    firsts[3] = piece_of("first", rows_first, 3)
    add_two(0)

    step0[3] = slot(firsts[3])
    add_two(1)
    with jax.named_scope("projected"):
        projected = late_use(projected).astype(jnp.bfloat16)
        projected = lax.all_gather(projected, "tensor", axis=0, tiled=True)
    projected = late_use(projected)
    up_terms = []
    for b in range(local_blocks):
        rows = slice(b * ROWS_BLK, (b + 1) * ROWS_BLK)
        term = SCALE * lax.dot_general(
            projected[rows], grad_out[rows], (((0,), (0,)), ((), ())), preferred_element_type=jnp.float32
        )
        up_terms.append(do(term.astype(jnp.bfloat16)))

    moved_terms = [slot(up_terms[0])]
    add_two(2)
    pin(mid1[0])

    moved_terms.append(slot(up_terms[1]))
    add_one(0)
    pin(mid1[1])
    owner_of = late_use(owner_of)
    onehot = (block_tenant[None, :] == tenant_ids[:, None]).astype(jnp.float32)
    inverse = 1.0 / jnp.sum(onehot, axis=1)
    same_owner = owner_of[:, None] == owner_of[None, :]
    earlier = tenant_ids[None, :] < tenant_ids[:, None]
    slot_of = owner_of * OWN_MAX + jnp.sum(jnp.logical_and(same_owner, earlier), axis=1)
    own_slots = z * OWN_MAX + jnp.arange(OWN_MAX, dtype=jnp.int32)
    ownership = (slot_of[None, :] == own_slots[:, None]).astype(jnp.float32)
    own_scale = jnp.sum(ownership * inverse[None, :], axis=1)
    block_slot = jnp.sum(
        jnp.where(block_tenant[:, None] == tenant_ids[None, :], slot_of[None, :], 0), axis=1
    ).reshape(dp_count, local_blocks)

    def hits(slots, batch):
        theirs = lax.dynamic_index_in_dim(block_slot, jnp.clip(batch, 0, 3), 0, keepdims=False)
        return (slots[:, None] == theirs[None, :]).astype(jnp.float32)

    def slots_at(where):
        return where * OWN_MAX + jnp.arange(OWN_MAX, dtype=jnp.int32)

    side = jnp.where(z == 1, 1, -1)
    far_hits = jnp.concatenate([hits(slots_at(z + 2 * side), z), hits(slots_at(z + 2 * side), z - side)], axis=1)
    near_hits = jnp.concatenate([hits(slots_at(z + side), z), hits(slots_at(z + side), z - side)], axis=1)
    last_hits = hits(slots_at(jnp.where(z == 2, 3, 0)), z)
    own_hits = jnp.concatenate([hits(own_slots, z), hits(own_slots, z - side)], axis=1) * own_scale[:, None]


    step1[0] = slot(twos[0])
    pin(mid1[2])
    add_two(3)
    back_part = do(backward(late_use(own_ids), grad_out, adapter_up))
    with jax.named_scope("back_proj"):
        back_full = jnp.where((jnp.arange(dp_count) == z)[:, None, None], back_part.now, 0.0)
        back_full = lax.psum(back_full, ("dp", "tensor"))

    step1[1] = slot(twos[1])

    def terms():
        return [held.now[None] for held in (*up_terms, *moved_terms)]

    with jax.named_scope("far_terms"):
        far_sums = do(combine(late_use(far_hits), terms(), jnp.bfloat16))
        far_terms = Held(middle_hop(far_sums.now))
    pin(mid1[3])

    step2[0] = slot(ones[0], first_and_last_hop)
    add_late(0)
    add_one(1)

    step1[2] = slot(twos[2])
    add_late(1)
    pin(far_terms)
    with jax.named_scope("last_terms"):
        unit = jnp.ones((OWN_MAX,), jnp.float32)
        last_sums = do(combine(late_use(last_hits), terms()[:local_blocks], jnp.bfloat16, unit, [far_terms.now]))
        last_terms = Held(last_hop(last_sums.now))

    step1[3] = slot(twos[3])
    with jax.named_scope("near_terms"):
        near_sums = do(combine(late_use(near_hits), terms(), jnp.bfloat16))
        near_terms = Held(middle_hop(near_sums.now))
    pin(mid2[0])
    add_one(2)

    step2[1] = slot(ones[1], first_and_last_hop)
    pin(mid2[1])
    add_late(2)
    add_one(3)

    step2[2] = slot(ones[2], first_and_last_hop)
    pin(last_terms)
    add_late(3)
    backs = (SCALE * late_use(back_full)).astype(jnp.bfloat16)
    backs = [lax.dynamic_index_in_dim(backs, order[n], 0, keepdims=False) for n in range(dp_count)]
    grad_down = do(
        down_gradient(
            index, ids, inverse, [rows_first, rows_two, rows_one, rows_late], backs, adapter_down.shape
        )
    )

    step2[3] = slot(ones[3], first_and_last_hop)
    slot_gate[:] = chain[-2:-1]
    grad_up = do(combine(late_use(own_hits), terms(), jnp.float32, own_scale, [near_terms.now, last_terms.now]))
    own_mask = jnp.broadcast_to(
        (late_use(own_ids)[:, None] == tenant_ids[None, :])[:, None, :, None],
        (local_blocks, ROWS_BLK, tenants, rank_width),
    )
    wide = jnp.where(
        own_mask, projected.reshape(local_blocks, ROWS_BLK, 1, rank_width), jnp.zeros((), jnp.bfloat16)
    ).reshape(batch_rows, tenants * rank_width)
    layer_out = jnp.zeros((batch_rows, hidden), jnp.bfloat16)
    for j, (start, tiles) in enumerate(pieces):
        total = SCALE * jnp.dot(
            wide, flat_up[:, start * tile : (start + tiles) * tile], preferred_element_type=jnp.float32
        )
        total = total + jnp.where(outer, lates[j].now, firsts[j].now).astype(jnp.float32)
        total = total + mid2[j].now.astype(jnp.float32)
        total = total + step2[j].now.astype(jnp.float32)
        layer_out = lax.dynamic_update_slice(layer_out, total.astype(jnp.bfloat16), (0, start * tile))
    return (layer_out, grad_down.now, grad_up.now)


def local_plain(tokens, up_weight, adapter_down, adapter_up, grad_out, block_tenant, owner_of):
    dp_count = lax.axis_size("dp")
    dp_index = lax.axis_index("dp")
    tp_index = lax.axis_index("tensor")
    seq_rows, feature_count = tokens.shape
    batch_rows = grad_out.shape[0]
    local_blocks = batch_rows // ROWS_BLK
    all_blocks = local_blocks * dp_count
    column_part = feature_count // dp_count
    slice_cols = adapter_down.shape[2]
    rank_width = adapter_down.shape[1]
    tenants = adapter_down.shape[0]
    gathered = lax.all_gather(tokens, "tensor", axis=0, tiled=True)
    spread = lax.all_to_all(
        gathered.reshape(1, batch_rows, dp_count, column_part),
        "dp",
        split_axis=2,
        concat_axis=0,
        tiled=True,
    )
    all_rows = spread.reshape(dp_count * batch_rows, column_part)
    base_out = lax.psum_scatter(
        jnp.dot(all_rows, up_weight, preferred_element_type=jnp.float32).astype(jnp.bfloat16),
        "dp",
        scatter_dimension=0,
        tiled=True,
    ).astype(jnp.float32)
    slice_start = tp_index * slice_cols
    feature_slice = lax.dynamic_slice_in_dim(all_rows, slice_start, slice_cols, 1).reshape(
        all_blocks, ROWS_BLK, slice_cols
    )
    down_blocks = jnp.take(adapter_down, block_tenant, axis=0)
    proj_part = jnp.einsum(
        "nrd,nkd->nrk", feature_slice, down_blocks, preferred_element_type=jnp.float32
    )
    local_ids = lax.dynamic_slice_in_dim(block_tenant, dp_index * local_blocks, local_blocks, 0)
    up_mine = jnp.take(adapter_up, local_ids, axis=0)
    out_blocks = grad_out.reshape(local_blocks, ROWS_BLK, grad_out.shape[1])
    back_part = jnp.einsum("nrf,nkf->nrk", out_blocks, up_mine, preferred_element_type=jnp.float32)
    back_full = lax.dynamic_update_slice_in_dim(
        jnp.zeros((all_blocks, ROWS_BLK, rank_width), jnp.float32),
        back_part,
        dp_index * local_blocks,
        0,
    )
    proj_sum, back_sum = lax.psum(
        (proj_part.reshape(-1, 2 * rank_width), back_full.reshape(-1, 2 * rank_width)),
        ("dp", "tensor"),
    )
    projected = proj_sum.reshape(all_blocks, ROWS_BLK, rank_width).astype(jnp.bfloat16)
    back_proj = (SCALE * back_sum).reshape(all_blocks, ROWS_BLK, rank_width).astype(jnp.bfloat16)
    proj_mine = lax.dynamic_slice_in_dim(projected, dp_index * local_blocks, local_blocks, 0)
    adapter_term = jnp.einsum(
        "nrk,nkf->nrf", proj_mine, up_mine, preferred_element_type=jnp.float32
    ).reshape(batch_rows, -1)
    layer_out = (base_out + SCALE * adapter_term).astype(jnp.bfloat16)
    down_terms = jnp.einsum(
        "nrk,nrd->nkd", back_proj, feature_slice, preferred_element_type=jnp.float32
    )
    tenant_ids = jnp.arange(tenants, dtype=jnp.int32)
    onehot = (block_tenant[None, :] == tenant_ids[:, None]).astype(jnp.float32)
    inverse = 1.0 / jnp.sum(onehot, axis=1)
    grad_down = (
        jnp.einsum("tn,nkd->tkd", onehot, down_terms, precision=lax.Precision.HIGHEST)
        * inverse[:, None, None]
    )
    up_terms = SCALE * jnp.einsum(
        "nrk,nrf->nkf", proj_mine, out_blocks, preferred_element_type=jnp.float32
    )
    same_owner = owner_of[:, None] == owner_of[None, :]
    earlier = tenant_ids[None, :] < tenant_ids[:, None]
    rank_in = jnp.sum(jnp.logical_and(same_owner, earlier), axis=1)
    slot_of = owner_of * OWN_MAX + rank_in
    own_slots = dp_index * OWN_MAX + jnp.arange(OWN_MAX, dtype=jnp.int32)
    ownership = (slot_of[None, :] == own_slots[:, None]).astype(jnp.float32)
    own_scale = jnp.dot(ownership, inverse, precision=lax.Precision.HIGHEST)
    total_slots = dp_count * OWN_MAX
    local_slots = jnp.take(slot_of, local_ids, axis=0)
    placement = (local_slots[None, :] == jnp.arange(total_slots, dtype=jnp.int32)[:, None]).astype(
        jnp.float32
    )
    buffer = jnp.einsum("sn,nkf->skf", placement, up_terms, precision=lax.Precision.HIGHEST)
    summed = lax.psum_scatter(
        buffer.astype(jnp.bfloat16), "dp", scatter_dimension=0, tiled=True
    ).astype(jnp.float32)
    grad_up = summed * own_scale[:, None, None]
    return (layer_out, grad_down, grad_up)


def solution(mesh):
    placed = (
        P(("groups", "dp", "tensor"), None),
        P("dp", "tensor"),
        P("groups", None, ("dp", "tensor")),
        P("groups", None, "tensor"),
        P(("groups", "dp"), "tensor"),
        P("groups"),
        P("groups"),
    )
    return jax.shard_map(
        local if mesh.shape["dp"] == 4 else local_plain,
        mesh=mesh,
        in_specs=placed,
        out_specs=(
            P(("groups", "dp"), "tensor"),
            P("groups", None, ("dp", "tensor")),
            P(("groups", "dp"), None, "tensor"),
        ),
        check_vma=False,
    )
```

```python
import functools

import jax
import jax.numpy as jnp
from jax import lax
from jax.experimental import pallas as pl
from jax.experimental.pallas import tpu as pltpu
from jax.sharding import PartitionSpec as P

ROWS_BLK = 128
OWN_MAX = 2
SCALE = 0.5
SPLIT = ((0, 2), (2, 5), (5, 9), (9, 13))
WINDOW = 2
FULL = 5
VMEM = 60 * 1024 * 1024
ANY = pl.BlockSpec(memory_space=pl.ANY)
SMEM = pl.BlockSpec(memory_space=pltpu.SMEM)


class Held:
    def __init__(self, now):
        self.now = now


def tie(*held):
    distinct = list({id(one): one for one in held}.values())
    for one, now in zip(distinct, lax.optimization_barrier(tuple(one.now for one in distinct))):
        one.now = now


def after(value, *earlier):
    return lax.optimization_barrier((value, *earlier))[0]


def across(value, axis, bit):
    count = lax.axis_size(axis)
    return lax.ppermute(value, axis, [(i, i ^ bit) for i in range(count)])


def outward(value, hop):
    last = lax.axis_size("dp") - 1
    return lax.ppermute(value, "dp", [(hop, hop + 1), (last - hop, last - hop - 1)])


def bits_of(count):
    return [1 << k for k in reversed(range(count.bit_length() - 1))]


def gather_rows(rows):
    held = [(0, rows)]
    for bit in bits_of(lax.axis_size("tensor")):
        held = held + [(mask | bit, across(value, "tensor", bit)) for mask, value in held]
    return held


def sum_over_tensor(value):
    for bit in bits_of(lax.axis_size("tensor")):
        value = value + across(value, "tensor", bit)
    return value


def tile_of(width):
    return 512 if width % 512 == 0 else 128


def cut(width):
    tiles = width // tile_of(width)
    counts = [tiles * (i + 1) // 13 - tiles * i // 13 for i in range(13)]
    counts = [sum(counts[a:b]) for a, b in SPLIT]
    edges = [0]
    for n in counts:
        edges.append(edges[-1] + n)
    return list(zip(edges[:-1], counts))


def call(kernel, flops, **kwargs):
    return pl.pallas_call(
        kernel,
        compiler_params=pltpu.CompilerParams(vmem_limit_bytes=VMEM),
        cost_estimate=pl.CostEstimate(flops=10 * flops, bytes_accessed=0, transcendentals=0),
        **kwargs,
    )


def share_kernel(masks, has_add, deps, index, *refs):
    blocks, refs = refs[: len(masks)], refs[len(masks) :]
    weight, refs = refs[0], refs[1:]
    if has_add:
        arrived, refs = refs[0], refs[1:]
    out = refs[deps]
    batch = blocks[0]
    if len(masks) > 1:
        batch = refs[deps + 1]
        rows = blocks[0].shape[0]

        @pl.when(pl.program_id(0) == 0)
        def _():
            for mask, block in zip(masks, blocks):
                first = pl.multiple_of((index[0] ^ mask) * rows, rows)
                batch[pl.ds(first, rows), :] = block[...]

    value = jnp.dot(batch[...], weight[...], preferred_element_type=jnp.float32)
    if has_add:
        value = value + arrived[...].astype(jnp.float32)
    out[...] = value.astype(jnp.bfloat16)


def share(index, gathered, weight, piece, arrived=None, deps=()):
    masks, blocks = zip(*gathered)
    rows, depth = blocks[0].shape
    batch_rows = rows * len(blocks)
    tile = tile_of(weight.shape[1])
    first, count = piece
    column = pl.BlockSpec((batch_rows, tile), lambda i, s: (0, i))
    has_add = arrived is not None
    return call(
        functools.partial(share_kernel, masks, has_add, len(deps)),
        2 * batch_rows * depth * count * tile,
        out_shape=jax.ShapeDtypeStruct((batch_rows, count * tile), jnp.bfloat16),
        grid_spec=pltpu.PrefetchScalarGridSpec(
            num_scalar_prefetch=1,
            grid=(count,),
            in_specs=[pl.BlockSpec((rows, depth), lambda i, s: (0, 0))] * len(blocks)
            + [pl.BlockSpec((depth, tile), lambda i, s: (0, first + i))]
            + [column] * has_add
            + [ANY] * len(deps),
            out_specs=column,
            scratch_shapes=[pltpu.VMEM((batch_rows, depth), jnp.bfloat16)] * (len(blocks) > 1),
        ),
    )(index, *blocks, weight, *([arrived] if has_add else []), *deps)


def pair_kernel(deps, one, other, weight, arrived_one, arrived_other, *refs):
    out_one, out_other, batch = refs[deps:]
    rows = one.shape[0]

    @pl.when(pl.program_id(0) == 0)
    def _():
        batch[:rows, :] = one[...]
        batch[rows:, :] = other[...]

    value = jnp.dot(batch[...], weight[...], preferred_element_type=jnp.float32)
    out_one[...] = (value[:rows] + arrived_one[...].astype(jnp.float32)).astype(jnp.bfloat16)
    out_other[...] = (value[rows:] + arrived_other[...].astype(jnp.float32)).astype(jnp.bfloat16)


def pair(one, other, weight, piece, arrived_one, arrived_other, deps):
    rows, depth = one.shape
    tile = tile_of(weight.shape[1])
    first, count = piece
    column = pl.BlockSpec((rows, tile), lambda i: (0, i))
    whole = pl.BlockSpec((rows, depth), lambda i: (0, 0))
    return call(
        functools.partial(pair_kernel, len(deps)),
        4 * rows * depth * count * tile,
        out_shape=[jax.ShapeDtypeStruct((rows, count * tile), jnp.bfloat16)] * 2,
        grid=(count,),
        in_specs=[whole, whole, pl.BlockSpec((depth, tile), lambda i: (0, first + i)), column, column] + [ANY] * len(deps),
        out_specs=[column] * 2,
        scratch_shapes=[pltpu.VMEM((2 * rows, depth), jnp.bfloat16)],
    )(one, other, weight, arrived_one, arrived_other, *deps)


def forward_kernel(count, deps, ids, *refs):
    blocks, down, outs = refs[:count], refs[count], refs[count + 1 + deps :]
    slices, _, _, width = down.shape
    for d in range(count):
        outs[d][...] = sum(
            lax.dot_general(
                blocks[d][:, n * width : (n + 1) * width],
                down[n, ids[d]],
                (((1,), (1,)), ((), ())),
                preferred_element_type=jnp.float32,
            )
            for n in range(slices)
        )


def forward(ids, blocks, down, deps):
    rows = blocks[0].shape[0]
    rank_width = down.shape[2]
    whole = pl.BlockSpec(memory_space=pltpu.VMEM)
    return call(
        functools.partial(forward_kernel, len(blocks), len(deps)),
        2 * len(blocks) * blocks[0].size * rank_width * 4,
        out_shape=[jax.ShapeDtypeStruct((rows, rank_width), jnp.float32)] * len(blocks),
        in_specs=[SMEM] + [whole] * (len(blocks) + 1) + [ANY] * len(deps),
        out_specs=[whole] * len(blocks),
    )(ids, *blocks, down, *deps)


def backward_kernel(ids, grad, up, out):
    @pl.when(pl.program_id(0) == 0)
    def _():
        out[...] = jnp.zeros_like(out)

    for b in range(grad.shape[0] // ROWS_BLK):
        rows = slice(b * ROWS_BLK, (b + 1) * ROWS_BLK)
        out[rows, :] += lax.dot_general(
            grad[rows, :], up[ids[b]], (((1,), (1,)), ((), ())), preferred_element_type=jnp.float32
        )


def backward(ids, grad_out, adapter_up):
    batch_rows, hidden = grad_out.shape
    tenants, rank_width, _ = adapter_up.shape
    tile = hidden // 4
    return call(
        backward_kernel,
        2 * batch_rows * hidden * rank_width * 4,
        out_shape=jax.ShapeDtypeStruct((batch_rows, rank_width), jnp.float32),
        grid_spec=pltpu.PrefetchScalarGridSpec(
            num_scalar_prefetch=1,
            grid=(hidden // tile,),
            in_specs=[
                pl.BlockSpec((batch_rows, tile), lambda i, n: (0, i)),
                pl.BlockSpec((tenants, rank_width, tile), lambda i, n: (0, 0, i)),
            ],
            out_specs=pl.BlockSpec((batch_rows, rank_width), lambda i, n: (0, 0)),
        ),
    )(ids, grad_out, adapter_up)


def down_kernel(masks, index, ids, inverse, *refs):
    out = refs[-1]
    out[...] = jnp.zeros_like(out)
    at = 0
    backs, refs = refs[: len(masks)], refs[len(masks) :]
    local_blocks = backs[0].shape[0] // ROWS_BLK
    for d, parts in enumerate(masks):
        for mask in parts:
            rows = refs[at].shape[0]
            first = 0 if len(parts) == 1 else pl.multiple_of((index[0] ^ mask) * rows, rows)
            step = min(rows, ROWS_BLK)
            for k in range(0, rows, step):
                tenant = ids[d * local_blocks + (first + k) // ROWS_BLK]
                out[tenant] += lax.dot_general(
                    backs[d][pl.ds(first + k, step), :],
                    refs[at][k : k + step, :],
                    (((0,), (0,)), ((), ())),
                    preferred_element_type=jnp.float32,
                )
            at += 1
    for n in range(out.shape[0]):
        out[n] *= inverse[n]


def down_gradient(index, ids, inverse, gathered, backs, shape):
    masks = [[mask for mask, _ in parts] for parts in gathered]
    arrays = [value for parts in gathered for _, value in parts]
    slice_cols = shape[2]
    return call(
        functools.partial(down_kernel, masks),
        8 * shape[1] * slice_cols * sum(value.shape[0] for value in arrays),
        out_shape=jax.ShapeDtypeStruct(shape, jnp.float32),
        grid_spec=pltpu.PrefetchScalarGridSpec(
            num_scalar_prefetch=2,
            grid=(1,),
            in_specs=[SMEM]
            + [pl.BlockSpec(back.shape, lambda i, s, n: (0, 0)) for back in backs]
            + [pl.BlockSpec((value.shape[0], slice_cols), lambda i, s, n: (0, s[0])) for value in arrays],
            out_specs=pl.BlockSpec(shape, lambda i, s, n: (0, 0, 0)),
        ),
    )(index, ids, inverse, *backs, *arrays)


def combine_kernel(count, extras, weights, scale, *refs):
    terms, more, out = refs[:count], refs[count : count + extras], refs[count + extras]
    parts = [term[0].astype(jnp.float32) for term in terms]
    for s in range(out.shape[0]):
        total = sum(part * weights[s, n] for n, part in enumerate(parts))
        if extras:
            total += sum(extra[s].astype(jnp.float32) for extra in more) * scale[s]
        out[s] = total.astype(out.dtype)


def combine(weights, terms, dtype, scale=None, extras=()):
    rank_width, hidden = terms[0].shape[1:]
    tile = hidden // 4
    slots = weights.shape[0]
    if scale is None:
        scale = jnp.ones((slots,), jnp.float32)
    return call(
        functools.partial(combine_kernel, len(terms), len(extras)),
        4 * slots * rank_width * hidden * len(terms),
        out_shape=jax.ShapeDtypeStruct((slots, rank_width, hidden), dtype),
        grid=(hidden // tile,),
        in_specs=[SMEM, SMEM]
        + [pl.BlockSpec((1, rank_width, tile), lambda i: (0, 0, i))] * len(terms)
        + [pl.BlockSpec((slots, rank_width, tile), lambda i: (0, 0, i))] * len(extras),
        out_specs=pl.BlockSpec((slots, rank_width, tile), lambda i: (0, 0, i)),
    )(weights, scale, *terms, *extras)


def local(tokens, up_weight, adapter_down, adapter_up, grad_out, block_tenant, owner_of):
    dp_count = 4
    z = lax.axis_index("dp")
    t = lax.axis_index("tensor")
    outer = jnp.logical_or(z == 0, z == 3)
    part_rows, feature_count = tokens.shape
    batch_rows, hidden = grad_out.shape
    local_blocks = batch_rows // ROWS_BLK
    depth = feature_count // dp_count
    tenants, rank_width, slice_cols = adapter_down.shape
    flat_up = adapter_up.reshape(tenants * rank_width, hidden)
    pieces = cut(hidden)
    tile = tile_of(hidden)
    index = t.reshape(1)

    def block_for(where):
        return lax.dynamic_slice_in_dim(tokens, where * depth, depth, 1)

    def first_hop(value):
        return lax.ppermute(value, "dp", [(0, 1), (3, 2)])

    def middle_hop(value):
        return lax.ppermute(value, "dp", [(1, 2), (2, 1)])

    def last_hop(value):
        return lax.ppermute(value, "dp", [(1, 0), (2, 3)])

    def first_and_last_hop(value):
        return lax.ppermute(value, "dp", [(0, 1), (3, 2), (1, 0), (2, 3)])

    def gather(value):
        return [(0, lax.all_gather(value, "tensor", axis=0, tiled=True))]

    down_all = lax.all_gather(adapter_down, "tensor", axis=0)
    far = lax.ppermute(block_for(z ^ 3), "dp", [(0, 3), (3, 0)])
    two = across(block_for(z ^ 2), "dp", 2)
    one = across(block_for(z ^ 1), "dp", 1)
    far, two, one = lax.optimization_barrier((far, two, one))
    middle = middle_hop(after(block_for(z ^ 3), far))
    mine = block_for(z)
    first_part = jnp.where(outer, far, mine)
    rows_first = gather_rows(first_part)

    chain = []
    work, earlier_work, pinned = [], [], []
    slot_gate = []

    def slot(value, hop=first_hop):
        k = len(chain)
        slot_gate[:] = chain[max(k - WINDOW, 0) : max(k - WINDOW + 1, 0)]
        with jax.named_scope(f"send{k}"):
            tie(value, *slot_gate, *pinned, *earlier_work)
            chain.append(Held(hop(value.now)))
        earlier_work[:] = work[-1:]
        pinned.clear()
        return chain[-1]

    def pin(arrived):
        pinned.append(arrived)

    def do(value):
        work.append(Held(value))
        return work[-1]

    def late_use(value):
        held = Held(value)
        tie(held, *slot_gate, *work[-1:])
        return held.now

    def piece_of(name, rows, j, arrived=None):
        arrived = arrived if arrived is None else arrived.now
        deps = [held.now for held in (*slot_gate, *work[-1:])]
        with jax.named_scope(f"{name}{j}"):
            return do(share(index, rows, up_weight, pieces[j], arrived=arrived, deps=deps))

    firsts, twos, ones, lates = {}, {}, {}, {}
    step0, step1, step2, mid1, mid2 = {}, {}, {}, {}, {}

    def add_two(j):
        twos[j] = piece_of("two", rows_two, j, step0[j])
        with jax.named_scope(f"mid_two{j}"):
            mid1[j] = Held(middle_hop(twos[j].now))

    def add_late(j):
        lates[j] = piece_of("late", rows_late, j, step1[j])
        with jax.named_scope(f"mid_late{j}"):
            mid2[j] = Held(middle_hop(lates[j].now))

    def add_one(j):
        ones[j] = piece_of("one", rows_one, j, mid1[j])

    def add_pair(j):
        with jax.named_scope(f"pair{j}"):
            deps = [held.now for held in (*slot_gate, *work[-1:])]
            lates[j], ones[j] = map(
                Held, pair(rows_late[0][1], rows_one[0][1], up_weight, pieces[j], step1[j].now, mid1[j].now, deps)
            )
            work.append(lates[j])
            mid2[j] = Held(middle_hop(lates[j].now))

    firsts[0] = piece_of("first", rows_first, 0)
    with jax.named_scope("two_rows"):
        two = late_use(two)
        rows_two = gather(two)

    step0[0] = slot(firsts[0])
    firsts[1] = piece_of("first", rows_first, 1)
    with jax.named_scope("one_rows"):
        one = late_use(one)
        rows_one = gather(one)
    with jax.named_scope("late_rows"):
        late_part = jnp.where(outer, mine, late_use(middle))
        rows_late = gather(late_part)
    block_tenant = late_use(block_tenant)

    step0[1] = slot(firsts[1])
    slot_gate[:] = chain[:1]
    firsts[2] = piece_of("first", rows_first, 2)

    slot_gate[:] = chain[1:2]
    tenant_ids = jnp.arange(tenants, dtype=jnp.int32)
    order = jnp.stack([jnp.where(outer, z ^ 3, z), z ^ 2, z ^ 1, jnp.where(outer, z, z ^ 3)])
    blocks_of = block_tenant.reshape(dp_count, local_blocks)
    ids = jnp.take(blocks_of, order, axis=0)
    row_ids = lax.dynamic_index_in_dim(ids, t * part_rows // ROWS_BLK, 1, keepdims=False)
    ids = ids.reshape(-1)
    own_ids = lax.dynamic_index_in_dim(blocks_of, z, 0, keepdims=False)
    with jax.named_scope("forward"):
        parts = jnp.stack(forward(late_use(row_ids), [first_part, two, one, late_part], down_all, ()))
        by_batch = jnp.where((order[None, :] == jnp.arange(dp_count)[:, None])[:, :, None, None], parts, 0.0)
        by_batch = do(jnp.sum(by_batch, axis=1)).now
        projected = lax.psum_scatter(by_batch, "dp", scatter_dimension=0, tiled=True)[0]

    step0[2] = slot(firsts[2])
    firsts[3] = piece_of("first", rows_first, 3)
    add_two(0)

    step0[3] = slot(firsts[3])
    with jax.named_scope("projected"):
        projected = late_use(projected).astype(jnp.bfloat16)
        projected = lax.all_gather(projected, "tensor", axis=0, tiled=True)
    add_two(1)
    projected = late_use(projected)
    up_terms = []
    for b in range(local_blocks):
        rows = slice(b * ROWS_BLK, (b + 1) * ROWS_BLK)
        term = SCALE * lax.dot_general(
            projected[rows], grad_out[rows], (((0,), (0,)), ((), ())), preferred_element_type=jnp.float32
        )
        up_terms.append(do(term.astype(jnp.bfloat16)))

    moved_terms = [slot(up_terms[0])]
    add_two(2)
    pin(mid1[0])

    moved_terms.append(slot(up_terms[1]))
    add_two(3)
    pin(mid1[1])
    owner_of = late_use(owner_of)
    onehot = (block_tenant[None, :] == tenant_ids[:, None]).astype(jnp.float32)
    inverse = 1.0 / jnp.sum(onehot, axis=1)
    same_owner = owner_of[:, None] == owner_of[None, :]
    earlier = tenant_ids[None, :] < tenant_ids[:, None]
    slot_of = owner_of * OWN_MAX + jnp.sum(jnp.logical_and(same_owner, earlier), axis=1)
    own_slots = z * OWN_MAX + jnp.arange(OWN_MAX, dtype=jnp.int32)
    ownership = (slot_of[None, :] == own_slots[:, None]).astype(jnp.float32)
    own_scale = jnp.sum(ownership * inverse[None, :], axis=1)
    block_slot = jnp.sum(
        jnp.where(block_tenant[:, None] == tenant_ids[None, :], slot_of[None, :], 0), axis=1
    ).reshape(dp_count, local_blocks)

    def hits(slots, batch):
        theirs = lax.dynamic_index_in_dim(block_slot, jnp.clip(batch, 0, 3), 0, keepdims=False)
        return (slots[:, None] == theirs[None, :]).astype(jnp.float32)

    def slots_at(where):
        return where * OWN_MAX + jnp.arange(OWN_MAX, dtype=jnp.int32)

    side = jnp.where(z == 1, 1, -1)
    far_hits = jnp.concatenate([hits(slots_at(z + 2 * side), z), hits(slots_at(z + 2 * side), z - side)], axis=1)
    near_hits = jnp.concatenate([hits(slots_at(z + side), z), hits(slots_at(z + side), z - side)], axis=1)
    last_hits = hits(slots_at(jnp.where(z == 2, 3, 0)), z)
    own_hits = jnp.concatenate([hits(own_slots, z), hits(own_slots, z - side)], axis=1) * own_scale[:, None]


    step1[0] = slot(twos[0])
    pin(mid1[2])
    add_one(0)
    back_part = do(backward(late_use(own_ids), grad_out, adapter_up))
    with jax.named_scope("back_proj"):
        back_full = jnp.where((jnp.arange(dp_count) == z)[:, None, None], back_part.now, 0.0)
        back_full = lax.psum(back_full, ("dp", "tensor"))

    step1[1] = slot(twos[1])

    def terms():
        return [held.now[None] for held in (*up_terms, *moved_terms)]

    with jax.named_scope("far_terms"):
        far_sums = do(combine(late_use(far_hits), terms(), jnp.bfloat16))
        far_terms = Held(middle_hop(far_sums.now))
    pin(mid1[3])

    step2[0] = slot(ones[0], first_and_last_hop)
    add_late(0)

    step1[2] = slot(twos[2])
    add_pair(1)
    pin(far_terms)
    with jax.named_scope("last_terms"):
        unit = jnp.ones((OWN_MAX,), jnp.float32)
        last_sums = do(combine(late_use(last_hits), terms()[:local_blocks], jnp.bfloat16, unit, [far_terms.now]))
        last_terms = Held(last_hop(last_sums.now))

    step1[3] = slot(twos[3])
    with jax.named_scope("near_terms"):
        near_sums = do(combine(late_use(near_hits), terms(), jnp.bfloat16))
        near_terms = Held(middle_hop(near_sums.now))
    pin(mid2[0])

    step2[1] = slot(ones[1], first_and_last_hop)
    pin(mid2[1])
    add_pair(2)

    step2[2] = slot(ones[2], first_and_last_hop)
    pin(last_terms)
    add_pair(3)
    backs = (SCALE * late_use(back_full)).astype(jnp.bfloat16)
    backs = [lax.dynamic_index_in_dim(backs, order[n], 0, keepdims=False) for n in range(dp_count)]
    grad_down = do(
        down_gradient(
            index, ids, inverse, [rows_first, rows_two, rows_one, rows_late], backs, adapter_down.shape
        )
    )

    step2[3] = slot(ones[3], first_and_last_hop)
    slot_gate[:] = chain[-2:-1]
    grad_up = do(combine(late_use(own_hits), terms(), jnp.float32, own_scale, [near_terms.now, last_terms.now]))
    own_mask = jnp.broadcast_to(
        (late_use(own_ids)[:, None] == tenant_ids[None, :])[:, None, :, None],
        (local_blocks, ROWS_BLK, tenants, rank_width),
    )
    wide = jnp.where(
        own_mask, projected.reshape(local_blocks, ROWS_BLK, 1, rank_width), jnp.zeros((), jnp.bfloat16)
    ).reshape(batch_rows, tenants * rank_width)
    layer_out = jnp.zeros((batch_rows, hidden), jnp.bfloat16)
    for j, (start, tiles) in enumerate(pieces):
        total = SCALE * jnp.dot(
            wide, flat_up[:, start * tile : (start + tiles) * tile], preferred_element_type=jnp.float32
        )
        total = total + jnp.where(outer, lates[j].now, firsts[j].now).astype(jnp.float32)
        total = total + mid2[j].now.astype(jnp.float32)
        total = total + step2[j].now.astype(jnp.float32)
        layer_out = lax.dynamic_update_slice(layer_out, total.astype(jnp.bfloat16), (0, start * tile))
    return (layer_out, grad_down.now, grad_up.now)


def local_plain(tokens, up_weight, adapter_down, adapter_up, grad_out, block_tenant, owner_of):
    dp_count = lax.axis_size("dp")
    dp_index = lax.axis_index("dp")
    tp_index = lax.axis_index("tensor")
    seq_rows, feature_count = tokens.shape
    batch_rows = grad_out.shape[0]
    local_blocks = batch_rows // ROWS_BLK
    all_blocks = local_blocks * dp_count
    column_part = feature_count // dp_count
    slice_cols = adapter_down.shape[2]
    rank_width = adapter_down.shape[1]
    tenants = adapter_down.shape[0]
    gathered = lax.all_gather(tokens, "tensor", axis=0, tiled=True)
    spread = lax.all_to_all(
        gathered.reshape(1, batch_rows, dp_count, column_part),
        "dp",
        split_axis=2,
        concat_axis=0,
        tiled=True,
    )
    all_rows = spread.reshape(dp_count * batch_rows, column_part)
    base_out = lax.psum_scatter(
        jnp.dot(all_rows, up_weight, preferred_element_type=jnp.float32).astype(jnp.bfloat16),
        "dp",
        scatter_dimension=0,
        tiled=True,
    ).astype(jnp.float32)
    slice_start = tp_index * slice_cols
    feature_slice = lax.dynamic_slice_in_dim(all_rows, slice_start, slice_cols, 1).reshape(
        all_blocks, ROWS_BLK, slice_cols
    )
    down_blocks = jnp.take(adapter_down, block_tenant, axis=0)
    proj_part = jnp.einsum(
        "nrd,nkd->nrk", feature_slice, down_blocks, preferred_element_type=jnp.float32
    )
    local_ids = lax.dynamic_slice_in_dim(block_tenant, dp_index * local_blocks, local_blocks, 0)
    up_mine = jnp.take(adapter_up, local_ids, axis=0)
    out_blocks = grad_out.reshape(local_blocks, ROWS_BLK, grad_out.shape[1])
    back_part = jnp.einsum("nrf,nkf->nrk", out_blocks, up_mine, preferred_element_type=jnp.float32)
    back_full = lax.dynamic_update_slice_in_dim(
        jnp.zeros((all_blocks, ROWS_BLK, rank_width), jnp.float32),
        back_part,
        dp_index * local_blocks,
        0,
    )
    proj_sum, back_sum = lax.psum(
        (proj_part.reshape(-1, 2 * rank_width), back_full.reshape(-1, 2 * rank_width)),
        ("dp", "tensor"),
    )
    projected = proj_sum.reshape(all_blocks, ROWS_BLK, rank_width).astype(jnp.bfloat16)
    back_proj = (SCALE * back_sum).reshape(all_blocks, ROWS_BLK, rank_width).astype(jnp.bfloat16)
    proj_mine = lax.dynamic_slice_in_dim(projected, dp_index * local_blocks, local_blocks, 0)
    adapter_term = jnp.einsum(
        "nrk,nkf->nrf", proj_mine, up_mine, preferred_element_type=jnp.float32
    ).reshape(batch_rows, -1)
    layer_out = (base_out + SCALE * adapter_term).astype(jnp.bfloat16)
    down_terms = jnp.einsum(
        "nrk,nrd->nkd", back_proj, feature_slice, preferred_element_type=jnp.float32
    )
    tenant_ids = jnp.arange(tenants, dtype=jnp.int32)
    onehot = (block_tenant[None, :] == tenant_ids[:, None]).astype(jnp.float32)
    inverse = 1.0 / jnp.sum(onehot, axis=1)
    grad_down = (
        jnp.einsum("tn,nkd->tkd", onehot, down_terms, precision=lax.Precision.HIGHEST)
        * inverse[:, None, None]
    )
    up_terms = SCALE * jnp.einsum(
        "nrk,nrf->nkf", proj_mine, out_blocks, preferred_element_type=jnp.float32
    )
    same_owner = owner_of[:, None] == owner_of[None, :]
    earlier = tenant_ids[None, :] < tenant_ids[:, None]
    rank_in = jnp.sum(jnp.logical_and(same_owner, earlier), axis=1)
    slot_of = owner_of * OWN_MAX + rank_in
    own_slots = dp_index * OWN_MAX + jnp.arange(OWN_MAX, dtype=jnp.int32)
    ownership = (slot_of[None, :] == own_slots[:, None]).astype(jnp.float32)
    own_scale = jnp.dot(ownership, inverse, precision=lax.Precision.HIGHEST)
    total_slots = dp_count * OWN_MAX
    local_slots = jnp.take(slot_of, local_ids, axis=0)
    placement = (local_slots[None, :] == jnp.arange(total_slots, dtype=jnp.int32)[:, None]).astype(
        jnp.float32
    )
    buffer = jnp.einsum("sn,nkf->skf", placement, up_terms, precision=lax.Precision.HIGHEST)
    summed = lax.psum_scatter(
        buffer.astype(jnp.bfloat16), "dp", scatter_dimension=0, tiled=True
    ).astype(jnp.float32)
    grad_up = summed * own_scale[:, None, None]
    return (layer_out, grad_down, grad_up)


def solution(mesh):
    placed = (
        P(("groups", "dp", "tensor"), None),
        P("dp", "tensor"),
        P("groups", None, ("dp", "tensor")),
        P("groups", None, "tensor"),
        P(("groups", "dp"), "tensor"),
        P("groups"),
        P("groups"),
    )
    return jax.shard_map(
        local if mesh.shape["dp"] == 4 else local_plain,
        mesh=mesh,
        in_specs=placed,
        out_specs=(
            P(("groups", "dp"), "tensor"),
            P("groups", None, ("dp", "tensor")),
            P(("groups", "dp"), None, "tensor"),
        ),
        check_vma=False,
    )
```
